256 devices in a mesh: ctx: 32 (over y, z), head: 8 (over x, core).
Axes of the slice: x: 4, y: 4, z: 8, core: 2. Of those that a mesh axis runs over, the one named last changes fastest.
Arguments:
- hidden: bfloat16 [512, 4096], P('head', 'ctx'), may hold values from -60 to 60
- norm_gain: float32 [4096], P('ctx'), may hold values from 0.1 to 1.9
- w_qkv: bfloat16 [4096, 6144], P('ctx'), may hold values from -0.09375 to 0.09375
- positions: int32 [512], replicated, may hold values from 0 to 1022, as said below
- cache_keys: bfloat16 [131072, 1024], P('ctx', 'head'), may hold values from -450 to 450
- cache_values: bfloat16 [131072, 1024], P('ctx', 'head'), may hold values from -6 to 6
- key_counts: int32 [32], P('ctx'), may hold values from 2048 to 4096, as said below
- w_out: bfloat16 [4096, 4096], P('head', 'ctx'), may hold values from -6 to 6
Outputs:
- attn_proj: bfloat16 [512, 4096], P('head', 'ctx')
The draws below stay inside these ranges and needn't reach their ends.
Inputs may be any that keep to these rules, and one draw needn't show every extreme that they name: Rows of the question have positions that start at 0 and rise by 1 to 3 from one row to the next; the last row stands at position 1022; cached keys were rotated at positions relative to the same anchor. In context block c only the first key_counts[c] of its 4096 rows are valid; in every draw some block is full.
All inputs are finite; a program needn't handle non-finite values.
Results may differ from the reference program's by a relative error of at most 0.0055.
The reference program's roundings to bfloat16 on the way count: a program that leaves them out, or rounds other values in their place, can miss the bound.
Values may be sent and summed in bfloat16 or wider, within the bound.
No kernel may reach another device: no remote copies, remote signals or barrier semaphores. Data moves between devices by JAX's collectives and lax.ppermute only.
A program may use at most 64 MiB of HBM per device.

```python
import math
import jax
import jax.numpy as jnp
from jax import lax

D = 4096
HEADS = 32
KV_HEADS = 8
HEAD_DIM = 128
KEYS_DEV = 4096
TQ = 512
KEYS = 131072
QKV = 6144
N_CTX = 32


def draw_hidden(key, part):
    col_pos = jnp.arange(D, dtype=jnp.float32) / (D - 1)
    base_vals = jnp.clip(jax.random.normal(key, (TQ, D), jnp.float32), -5.0, 5.0)
    values_out = base_vals * (0.6 * 3.0 ** col_pos)[None, :]
    return values_out.astype(jnp.bfloat16)


def draw_positions(key, part):
    pair_gaps = jax.random.randint(key, ((TQ - 2) // 2,), 1, 4)
    paired = jnp.stack([pair_gaps, 4 - pair_gaps], axis=1).reshape(-1)
    gap_sizes = jnp.concatenate([paired, jnp.full((1,), 2, jnp.int32)])
    return jnp.concatenate([jnp.zeros((1,), jnp.int32), jnp.cumsum(gap_sizes).astype(jnp.int32)]).astype(jnp.int32)


def draw_key_counts(key, part):
    key_one, key_two = jax.random.split(key)
    counts_out = jax.random.randint(key_one, (N_CTX,), KEYS_DEV // 2, KEYS_DEV + 1)
    full_group = jax.random.randint(key_two, (), 0, N_CTX)
    return counts_out.at[full_group].set(KEYS_DEV).astype(jnp.int32)


def draw_cache_keys(key, part):
    width_all = KV_HEADS * HEAD_DIM
    key_one = jax.random.fold_in(key, 0)
    base_vals = jnp.clip(jax.random.normal(key_one, (KEYS_DEV * N_CTX, width_all), jnp.float32), -6.0, 6.0)
    return base_vals.astype(jnp.bfloat16)


def steps_of(own_key, extent, cuts, low, high):
    gain, own = 1.0, jax.random.fold_in(own_key, 6)
    for dim, parts in cuts:
        heights = jnp.exp(jax.random.uniform(jax.random.fold_in(own, dim), (parts,), jnp.float32, low / len(cuts), high / len(cuts)))
        gain = gain * jnp.repeat(heights, extent[dim] // parts).reshape([-1 if axis == dim else 1 for axis in range(len(extent))])
    return gain


def scatter_about(rng, extent, width, bound, pieces=(), kind=jnp.bfloat16):
    entries = width * jax.random.normal(rng, extent, jnp.float32)
    if pieces:
        entries = entries * steps_of(rng, extent, pieces, -0.22, 0.18)
    return jnp.clip(entries, -bound, bound).astype(kind)


def setup_inputs(seed: int = 0) -> dict:
    key_of = jax.random.split(jax.random.key(seed), 9)
    return {
        "hidden": draw_hidden(jax.random.fold_in(key_of[8], 71), 0),
        "norm_gain": jnp.clip(1.0 + 0.18 * jax.random.normal(key_of[1], (D,), jnp.float32), 0.1, 1.9),
        "w_qkv": scatter_about(key_of[2], (D, QKV), D ** -0.5, 0.09375, ((0, 32),)),
        "positions": draw_positions(jax.random.fold_in(key_of[8], 71), 0),
        "cache_keys": draw_cache_keys(jax.random.fold_in(key_of[8], 71), 0),
        "cache_values": scatter_about(key_of[5], (KEYS, KV_HEADS * HEAD_DIM), 1.0, 6.0, ((0, 32), (1, 8))),
        "key_counts": draw_key_counts(jax.random.fold_in(key_of[8], 71), 0),
        "w_out": scatter_about(key_of[7], (HEADS * HEAD_DIM, D), 1.5, 6.0, ((0, 8), (1, 32))),
    }


NEG_FILL = -1e+30

def rotate(values_in, positions_in):
    half_dim = values_in.shape[-1] // 2
    frequency = 500000.0 ** (-(jnp.arange(half_dim, dtype=jnp.float32) * 2.0 / values_in.shape[-1]))
    angles = positions_in.astype(jnp.float32)[:, None] * frequency[None, :]
    angles = angles.reshape((angles.shape[0],) + (1,) * (values_in.ndim - 2) + (half_dim,))
    cosine = jnp.cos(angles)
    sine_val = jnp.sin(angles)
    first_half = values_in[..., :half_dim]
    second = values_in[..., half_dim:]
    return jnp.concatenate([first_half * cosine - second * sine_val, second * cosine + first_half * sine_val], axis=-1)

def attend(query_block, key_block, value_block, new_keys, new_values, cache_mask, self_mask):
    score_scale = 1.0 / math.sqrt(query_block.shape[-1])
    query_f = query_block.astype(jnp.float32)
    score_cache = jnp.einsum('tagh,kah->tagk', query_f, key_block.astype(jnp.float32)) * score_scale
    score_self = jnp.einsum('tagh,uah->tagu', query_f, new_keys.astype(jnp.float32)) * score_scale
    score_cache = jnp.where(cache_mask[None, None, None, :], score_cache, NEG_FILL)
    score_self = jnp.where(self_mask[:, None, None, :], score_self, NEG_FILL)
    row_max = jnp.maximum(lax.optimization_barrier(jnp.max(score_cache, axis=-1)), lax.optimization_barrier(jnp.max(score_self, axis=-1)))
    exp_cache = jnp.exp(score_cache - row_max[..., None]).astype(jnp.bfloat16)
    exp_self = jnp.exp(score_self - row_max[..., None]).astype(jnp.bfloat16)
    totals = lax.optimization_barrier(jnp.sum(exp_cache.astype(jnp.float32), axis=-1)) + lax.optimization_barrier(jnp.sum(exp_self.astype(jnp.float32), axis=-1))
    weighted = jnp.einsum('tagk,kah->tagh', exp_cache.astype(jnp.float32), value_block.astype(jnp.float32))
    weighted = weighted + jnp.einsum('tagu,uah->tagh', exp_self.astype(jnp.float32), new_values.astype(jnp.float32))
    return (row_max, totals, weighted)

def reference(hidden, norm_gain, w_qkv, positions, cache_keys, cache_values, key_counts, w_out):
    group_size = HEADS // KV_HEADS
    hidden_f = hidden.astype(jnp.float32)
    inv_rms = lax.rsqrt(lax.optimization_barrier(jnp.mean(hidden_f * hidden_f, axis=1)) + 1e-05)
    scaled = (hidden_f * norm_gain[None, :]).astype(jnp.bfloat16)
    mixed_cols = jnp.dot(scaled, w_qkv, preferred_element_type=jnp.float32) * inv_rms[:, None]
    mixed_cols = mixed_cols.reshape(TQ, KV_HEADS, group_size + 2, HEAD_DIM)
    turned = rotate(mixed_cols[:, :, :group_size + 1], positions)
    rotated = jnp.concatenate([turned, mixed_cols[:, :, group_size + 1:]], axis=2).astype(jnp.bfloat16)
    queries = rotated[:, :, :group_size]
    new_keys = rotated[:, :, group_size]
    new_values = rotated[:, :, group_size + 1]
    keys_all = cache_keys.reshape(N_CTX, KEYS_DEV, KV_HEADS, HEAD_DIM)
    values_all = cache_values.reshape(N_CTX, KEYS_DEV, KV_HEADS, HEAD_DIM)
    block_rows = math.gcd(TQ, 128)
    block_count = TQ // block_rows
    query_blocks = queries.reshape(block_count, block_rows, KV_HEADS, group_size, HEAD_DIM)
    block_starts = jnp.arange(block_count, dtype=jnp.int32) * block_rows

    def one_group(state_in, inputs):
        key_block, value_block, valid_count, group_index = inputs
        cache_mask = jnp.arange(KEYS_DEV, dtype=jnp.int32) < valid_count

        def one_block(block_args):
            query_block, row_start = block_args
            rows_here = row_start + jnp.arange(block_rows, dtype=jnp.int32)
            self_mask = (jnp.arange(TQ, dtype=jnp.int32)[None, :] <= rows_here[:, None]) & (group_index == 0)
            return attend(query_block, key_block, value_block, new_keys, new_values, cache_mask, self_mask)
        part_max, part_sum, part_out = lax.map(one_block, (query_blocks, block_starts))
        part_max = part_max.reshape(TQ, KV_HEADS, group_size)
        part_sum = part_sum.reshape(TQ, KV_HEADS, group_size)
        part_out = part_out.reshape(TQ, KV_HEADS, group_size, HEAD_DIM)
        max_a, sum_a, out_a = state_in
        joined_max = jnp.maximum(max_a, part_max)
        weight_a = jnp.exp(max_a - joined_max)
        weight_b = jnp.exp(part_max - joined_max)
        joined_sum = sum_a * weight_a + part_sum * weight_b
        joined_out = out_a * weight_a[..., None] + part_out * weight_b[..., None]
        return ((joined_max, joined_sum, joined_out), None)
    start_state = (jnp.full((TQ, KV_HEADS, group_size), NEG_FILL, jnp.float32), jnp.zeros((TQ, KV_HEADS, group_size), jnp.float32), jnp.zeros((TQ, KV_HEADS, group_size, HEAD_DIM), jnp.float32))
    group_ids = jnp.arange(N_CTX, dtype=jnp.int32)
    final_state, _ = lax.scan(one_group, start_state, (keys_all, values_all, key_counts, group_ids))
    final_max, final_sum, final_out = final_state
    attended = (final_out / final_sum[..., None]).astype(jnp.bfloat16).reshape(TQ, HEADS * HEAD_DIM)
    return jnp.dot(attended, w_out, preferred_element_type=jnp.float32).astype(jnp.bfloat16)
```

```python
import functools
import math

import jax
import jax.numpy as jnp
from jax import lax
from jax.experimental import pallas as pl
from jax.experimental.pallas import tpu as pltpu
from jax.sharding import Mesh
from jax.sharding import PartitionSpec as P

D = 4096
HEADS = 32
KV_HEADS = 8
HEAD_DIM = 128
GROUP = HEADS // KV_HEADS
SLOTS = GROUP + 2
TQ = 512
KEYS_DEV = 4096
NEG_FILL = -1e30
LOG2E = 1.4426950408889634

YN, ZN, XN, CN = 4, 8, 4, 2
HN = XN * CN
CTX = ("y", "z")
HEAD = ("x", "core")
OWN = 16
TAIL = 128
KTOT = KEYS_DEV + TAIL
OUT_W = 640
KEY_TILE = 512


def exchange(array, axes):
    return lax.all_to_all(array, axes, 0, 0, tiled=True)


def copies(array, count):
    return jnp.broadcast_to(array[None], (count, *array.shape))


def attend_kernel(info_ref, q_ref, k_ref, v_ref, new_ref, o_ref, kx, vx, scores, weights):
    count = info_ref[0]
    first_own = info_ref[1]
    rows = q_ref.shape[0]

    @pl.when(pl.program_id(0) == 0)
    def _():
        lane = lax.broadcasted_iota(jnp.int32, (KEYS_DEV, HEAD_DIM), 1)
        key_row = lax.broadcasted_iota(jnp.int32, (KEYS_DEV, HEAD_DIM), 0)
        kx[0:KEYS_DEV, 0:HEAD_DIM] = k_ref[...]
        kx[0:KEYS_DEV, HEAD_DIM:] = jnp.where((lane == 0) & (key_row >= count), NEG_FILL, 0.0).astype(jnp.bfloat16)
        vx[0:KEYS_DEV, 0:HEAD_DIM] = v_ref[...]
        vx[0:KEYS_DEV, HEAD_DIM:] = jnp.where(lane == 0, 1.0, 0.0).astype(jnp.bfloat16)
        kx[KEYS_DEV:, :] = jnp.zeros((TAIL, 2 * HEAD_DIM), jnp.bfloat16)
        vx[KEYS_DEV:, :] = jnp.zeros((TAIL, 2 * HEAD_DIM), jnp.bfloat16)
        kx[KEYS_DEV : KEYS_DEV + OWN, 0:HEAD_DIM] = new_ref[:, 0:HEAD_DIM]
        vx[KEYS_DEV : KEYS_DEV + OWN, 0:HEAD_DIM] = new_ref[:, HEAD_DIM:]
        vx[KEYS_DEV : KEYS_DEV + OWN, HEAD_DIM:] = jnp.where(lane[:OWN] == 0, 1.0, 0.0).astype(jnp.bfloat16)

    scale = 1.0 / math.sqrt(HEAD_DIM)
    one = jnp.where(lax.broadcasted_iota(jnp.int32, (rows, HEAD_DIM), 1) == 0, 1.0, 0.0).astype(jnp.bfloat16)
    qx = jnp.concatenate([q_ref[...], one], axis=1)
    row = lax.broadcasted_iota(jnp.int32, (rows, TAIL), 0)
    asked = ((row // OWN) % ZN) * (OWN * YN) + (row // (OWN * ZN)) * OWN + row % OWN
    own = lax.broadcasted_iota(jnp.int32, (rows, TAIL), 1)
    seen = (own < OWN) & (own + first_own <= asked)

    def product(a, b):
        return lax.dot_general(a, b, (((1,), (1,)), ((), ())), preferred_element_type=jnp.float32)

    top = jnp.where(seen, product(qx, kx[KEYS_DEV:, :]), NEG_FILL)
    scores[:, KEYS_DEV:] = top
    for start in range(0, KEYS_DEV, KEY_TILE):
        part = product(qx, kx[start : start + KEY_TILE, :])
        scores[:, start : start + KEY_TILE] = part
        for j in range(0, KEY_TILE, 128):
            top = jnp.maximum(top, part[:, j : j + 128])
    best = jnp.max(top, axis=1, keepdims=True)
    shift = best * (scale * LOG2E)
    for start in range(0, KTOT, 128):
        weights[:, start : start + 128] = jnp.exp2(
            scores[:, start : start + 128] * (scale * LOG2E) - shift
        ).astype(jnp.bfloat16)
    out = jnp.dot(weights[...], vx[...], preferred_element_type=jnp.float32)
    total = out[:, HEAD_DIM : HEAD_DIM + 1]
    o_ref[:, 0:HEAD_DIM] = (out[:, 0:HEAD_DIM] / total).astype(jnp.bfloat16)
    level = best * scale + jnp.log(total)
    high = level.astype(jnp.bfloat16)
    rest = level - high.astype(jnp.float32)
    mid = rest.astype(jnp.bfloat16)
    low = (rest - mid.astype(jnp.float32)).astype(jnp.bfloat16)
    lane = lax.broadcasted_iota(jnp.int32, (rows, HEAD_DIM), 1)
    packed = jnp.where(
        lane == 0,
        high.astype(jnp.float32),
        jnp.where(lane == 1, mid.astype(jnp.float32), jnp.where(lane == 2, low.astype(jnp.float32), 0.0)),
    )
    o_ref[:, HEAD_DIM:] = packed.astype(jnp.bfloat16)


def attend(info, queries, key_block, value_block, new_rows):
    rows = TQ
    return pl.pallas_call(
        attend_kernel,
        grid_spec=pltpu.PrefetchScalarGridSpec(
            num_scalar_prefetch=1,
            grid=(GROUP,),
            in_specs=[
                pl.BlockSpec((rows, HEAD_DIM), lambda s, info: (0, s)),
                pl.BlockSpec((KEYS_DEV, HEAD_DIM), lambda s, info: (0, 0)),
                pl.BlockSpec((KEYS_DEV, HEAD_DIM), lambda s, info: (0, 0)),
                pl.BlockSpec((OWN, 2 * HEAD_DIM), lambda s, info: (0, 0)),
            ],
            out_specs=pl.BlockSpec((rows, 2 * HEAD_DIM), lambda s, info: (0, s)),
            scratch_shapes=[
                pltpu.VMEM((KTOT, 2 * HEAD_DIM), jnp.bfloat16),
                pltpu.VMEM((KTOT, 2 * HEAD_DIM), jnp.bfloat16),
                pltpu.VMEM((rows, KTOT), jnp.float32),
                pltpu.VMEM((rows, KTOT), jnp.bfloat16),
            ],
        ),
        out_shape=jax.ShapeDtypeStruct((rows, GROUP * 2 * HEAD_DIM), jnp.bfloat16),
        compiler_params=pltpu.CompilerParams(vmem_limit_bytes=48 * 1024 * 1024),
        name="attend",
    )(info, queries, key_block, value_block, new_rows)


def rotate(values_in, positions_in):
    half = HEAD_DIM // 2
    frequency = 500000.0 ** (-(jnp.arange(half, dtype=jnp.float32) * 2.0 / HEAD_DIM))
    angles = positions_in.astype(jnp.float32)[:, None] * frequency[None, :]
    cosine = jnp.cos(angles)[:, None, :]
    sine = jnp.sin(angles)[:, None, :]
    first, second = values_in[..., :half], values_in[..., half:]
    return jnp.concatenate([first * cosine - second * sine, second * cosine + first * sine], axis=-1)


def per_device(hidden, norm_gain, w_qkv, positions, cache_keys, cache_values, key_counts, w_out):
    y, z = lax.axis_index("y"), lax.axis_index("z")
    head = lax.axis_index(HEAD)
    width = SLOTS * HEAD_DIM
    scaled = (hidden.astype(jnp.float32) * norm_gain[None, :]).astype(jnp.bfloat16)
    both = jnp.concatenate([hidden, scaled], axis=1).reshape(YN, 1, OWN, 256)
    sent = jnp.broadcast_to(both, (YN, HN, OWN, 256)).reshape(YN * HN, OWN, 256)
    own_columns = lax.dynamic_slice_in_dim(w_qkv, head * width, width, axis=1)
    w_all = exchange(copies(own_columns, YN), "y")
    got = exchange(sent, ("y", "x", "core")).reshape(YN, HN * OWN, 256)
    plain = got[:, :, :128].astype(jnp.float32)
    square = jnp.sum(plain * plain, axis=(0, 2))
    turned = jnp.moveaxis(got[:, :, 128:], 0, 1).reshape(HN * OWN, YN * 128)
    mix = jnp.dot(turned, w_all.reshape(YN * 128, width), preferred_element_type=jnp.float32)
    mix = jnp.concatenate([mix, jnp.broadcast_to(square[:, None], (HN * OWN, 128))], axis=1)
    share = jnp.sum(exchange(mix.reshape(ZN, OWN, width + 128), "z"), axis=0)
    inv_rms = lax.rsqrt(share[:, width] / D + 1e-05)
    share = (share[:, :width] * inv_rms[:, None]).reshape(OWN, SLOTS, HEAD_DIM)
    first_own = z * (OWN * YN) + y * OWN
    here = lax.dynamic_slice_in_dim(positions, first_own, OWN)
    turned = rotate(share[:, : GROUP + 1], here).astype(jnp.bfloat16)
    queries = turned[:, :GROUP].reshape(OWN, GROUP * HEAD_DIM)
    new_rows = jnp.concatenate([turned[:, GROUP], share[:, GROUP + 1].astype(jnp.bfloat16)], axis=1)
    queries = exchange(copies(queries, YN * ZN), CTX).reshape(TQ, GROUP * HEAD_DIM)
    info = jnp.stack([key_counts[0], first_own.astype(jnp.int32)])
    w_full = exchange(copies(w_out, HN), HEAD).reshape(HEADS * HEAD_DIM, 128)
    part = attend(info, queries, cache_keys, cache_values, new_rows)
    part = part.reshape(TQ, GROUP, 2, HEAD_DIM)
    levels = part[:, :, 1, :32].reshape(TQ, GROUP * 32)
    message = jnp.concatenate([part[:, :, 0].reshape(TQ, GROUP * HEAD_DIM), levels], axis=1)
    message = message.reshape(256, 2, OUT_W)
    back = exchange(message, ("y", "x", "core", "z"))
    back = back.reshape(YN, HN, ZN, 2, OUT_W).astype(jnp.float32)
    levels = back[..., GROUP * HEAD_DIM :].reshape(YN, HN, ZN, 2, GROUP, 32)
    level = levels[..., 0] + levels[..., 1] + levels[..., 2]
    outs = back[..., : GROUP * HEAD_DIM].reshape(YN, HN, ZN, 2, GROUP, HEAD_DIM)
    most = jnp.max(level, axis=(0, 2), keepdims=True)
    factor = jnp.exp(level - most)
    summed = jnp.sum(outs * factor[..., None], axis=(0, 2))
    total = jnp.sum(factor, axis=(0, 2))
    attended = (summed / total[..., None]).astype(jnp.bfloat16)
    attended = jnp.moveaxis(attended, 0, 1).reshape(2, HEADS * HEAD_DIM)
    rows = exchange(copies(attended, YN * ZN), CTX).reshape(64, HEADS * HEAD_DIM)
    return jnp.dot(rows, w_full, preferred_element_type=jnp.float32).astype(jnp.bfloat16)


def solution(mesh):
    fine = Mesh(mesh.devices.reshape(YN, ZN, XN, CN), ("y", "z", "x", "core"))
    return jax.shard_map(
        per_device,
        mesh=fine,
        in_specs=(
            P(HEAD, CTX),
            P(CTX),
            P(CTX, None),
            P(),
            P(CTX, HEAD),
            P(CTX, HEAD),
            P(CTX),
            P(HEAD, CTX),
        ),
        out_specs=P(HEAD, CTX),
        check_vma=False,
    )
```

```python
import math

import jax
import jax.numpy as jnp
from jax import lax
from jax.experimental import pallas as pl
from jax.experimental.pallas import tpu as pltpu
from jax.sharding import Mesh
from jax.sharding import PartitionSpec as P

D = 4096
HEADS = 32
KV_HEADS = 8
HEAD_DIM = 128
GROUP = HEADS // KV_HEADS
SLOTS = GROUP + 2
WIDTH = SLOTS * HEAD_DIM
FLAT = GROUP * HEAD_DIM
TQ = 512
KEYS_DEV = 4096
NEG_FILL = -1e30
SCALE = 1.0 / math.sqrt(HEAD_DIM)
SCALE2 = SCALE * 1.4426950408889634

YN, ZN, XN, CN = 4, 8, 4, 2
HN = XN * CN
CTXN = YN * ZN
CTX = ("y", "z")
HEAD = ("x", "core")
OWN = TQ // CTXN
TAIL = 128
KEY_TILE = 512
PAIR = 2

VMEM = pl.BlockSpec(memory_space=pltpu.VMEM)
SMEM = pl.BlockSpec(memory_space=pltpu.SMEM)
ANY = pl.BlockSpec(memory_space=pl.ANY)


def shape(dims, kind):
    return jax.ShapeDtypeStruct(dims, kind)


def params(mib):
    return pltpu.CompilerParams(vmem_limit_bytes=mib * 1024 * 1024)


def exchange(array, axes):
    return lax.all_to_all(array, axes, 0, 0, tiled=True)


def split_kernel(head_ref, hidden_ref, gain_ref, w_ref, sent_ref, own_ref, sem):
    first = pl.multiple_of(head_ref[0] * WIDTH, 128)
    copy = pltpu.make_async_copy(w_ref.at[:, pl.ds(first, WIDTH)], own_ref, sem)
    copy.start()
    hidden = hidden_ref[...]
    scaled = (hidden.astype(jnp.float32) * gain_ref[...]).astype(jnp.bfloat16)
    both = jnp.concatenate([hidden, scaled], axis=1)
    for y in range(YN):
        for h in range(HN):
            sent_ref[y * HN + h] = both[y * OWN : (y + 1) * OWN]
    copy.wait()


def project_kernel(info_ref, got_ref, w0, w1, w2, w3, table_ref, k_ref, v_ref, mix_ref):
    y = info_ref[2]
    total = None
    square = None
    for shift, w in enumerate((w0, w1, w2, w3)):
        source = lax.rem(y + YN - shift, YN)
        part = got_ref[pl.ds(source * HN, HN)].reshape(HN * OWN, 2 * HEAD_DIM)
        term = jnp.dot(part[:, HEAD_DIM:], w[...], preferred_element_type=jnp.float32)
        plain = part[:, :HEAD_DIM].astype(jnp.float32)
        own = jnp.sum(plain * plain, axis=1, keepdims=True)
        total = term if total is None else total + term
        square = own if square is None else square + own
    mix_ref[:, :, :WIDTH] = total.reshape(ZN, OWN, WIDTH)
    mix_ref[:, :, WIDTH:] = jnp.broadcast_to(square, (HN * OWN, HEAD_DIM)).reshape(ZN, OWN, HEAD_DIM)


def turn_kernel(mix_ref, table_ref, queries_ref, new_ref):
    share = mix_ref[0]
    for z in range(1, ZN):
        share = share + mix_ref[z]
    inv_rms = lax.rsqrt(share[:, WIDTH : WIDTH + 1] / D + 1e-05)
    cosine, sine = table_ref[:, :HEAD_DIM], table_ref[:, HEAD_DIM:]
    slots = []
    for s in range(SLOTS):
        value = share[:, s * HEAD_DIM : (s + 1) * HEAD_DIM] * inv_rms
        if s <= GROUP:
            value = value * cosine + pltpu.roll(value, HEAD_DIM // 2, 1) * sine
        slots.append(value.astype(jnp.bfloat16))
    queries = jnp.concatenate(slots[:GROUP], axis=1)
    for c in range(CTXN):
        queries_ref[c] = queries
    new_ref[...] = jnp.concatenate(slots[GROUP:], axis=1)


def attend_kernel(info_ref, q_ref, k_ref, v_ref, new_ref, o_ref):
    count = info_ref[0]
    first_own = info_ref[1]
    rows = PAIR * TQ

    def lane(n):
        return lax.broadcasted_iota(jnp.int32, (n, HEAD_DIM), 1)

    def first_lane(n):
        return jnp.where(lane(n) == 0, 1.0, 0.0).astype(jnp.bfloat16)

    def product(a, b):
        return lax.dot_general(a, b, (((1,), (1,)), ((), ())), preferred_element_type=jnp.float32)

    asked = lax.broadcasted_iota(jnp.int32, (rows, TAIL), 0) % TQ
    own = lax.broadcasted_iota(jnp.int32, (rows, TAIL), 1)
    seen = (own < OWN) & (own + first_own <= asked)
    blank = jnp.zeros((TAIL - OWN, HEAD_DIM), jnp.bfloat16)
    tail_keys = jnp.concatenate([new_ref[:, :HEAD_DIM], blank], axis=0)
    tail_values = jnp.concatenate([new_ref[:, HEAD_DIM:], blank], axis=0)
    spot = lane(TQ)
    packed = jnp.zeros((TQ, HEAD_DIM), jnp.float32)
    for pair in range(GROUP // PAIR):
        slots = range(pair * PAIR, (pair + 1) * PAIR)
        queries = jnp.concatenate(
            [q_ref[:, :, s * HEAD_DIM : (s + 1) * HEAD_DIM].reshape(TQ, HEAD_DIM) for s in slots], axis=0
        )
        wide = jnp.concatenate([queries, first_lane(rows)], axis=1)
        best = jnp.full((rows, 1), NEG_FILL, jnp.float32)
        sums = jnp.zeros((rows, 2 * HEAD_DIM), jnp.float32)
        for start in range(0, KEYS_DEV + TAIL, KEY_TILE):
            if start < KEYS_DEV:
                index = lax.broadcasted_iota(jnp.int32, (KEY_TILE, HEAD_DIM), 0) + start
                hide = jnp.where((lane(KEY_TILE) == 0) & (index >= count), NEG_FILL, 0.0).astype(jnp.bfloat16)
                keys = jnp.concatenate([k_ref[start : start + KEY_TILE, :], hide], axis=1)
                values = jnp.concatenate([v_ref[start : start + KEY_TILE, :], first_lane(KEY_TILE)], axis=1)
                scores = product(wide, keys)
            else:
                values = jnp.concatenate([tail_values, first_lane(TAIL)], axis=1)
                scores = jnp.where(seen, product(queries, tail_keys), NEG_FILL)
            higher = jnp.maximum(best, jnp.max(scores, axis=1, keepdims=True))
            weights = jnp.exp2(scores * SCALE2 - higher * SCALE2).astype(jnp.bfloat16)
            sums = sums * jnp.exp2((best - higher) * SCALE2) + jnp.dot(
                weights, values, preferred_element_type=jnp.float32
            )
            best = higher
        total = sums[:, HEAD_DIM : HEAD_DIM + 1]
        outs = (sums[:, :HEAD_DIM] * (1.0 / total)).astype(jnp.bfloat16)
        level = best * SCALE + jnp.log(total)
        high = level.astype(jnp.bfloat16).astype(jnp.float32)
        mid = (level - high).astype(jnp.bfloat16).astype(jnp.float32)
        low = (level - high) - mid
        for n, s in enumerate(slots):
            here = slice(n * TQ, (n + 1) * TQ)
            o_ref[:, :, s * HEAD_DIM : (s + 1) * HEAD_DIM] = outs[here].reshape(CTXN, OWN, HEAD_DIM)
            for step, piece in enumerate((high, mid, low)):
                packed = jnp.where(spot == step * GROUP + s, piece[here], packed)
    o_ref[:, :, FLAT:] = packed.astype(jnp.bfloat16).reshape(CTXN, OWN, HEAD_DIM)


def join_kernel(back_ref, rows_ref):
    parts = back_ref[:, :, FLAT:].astype(jnp.float32).reshape(CTXN * OWN, HEAD_DIM)
    level = parts + pltpu.roll(parts, HEAD_DIM - GROUP, 1) + pltpu.roll(parts, HEAD_DIM - 2 * GROUP, 1)
    spot = lax.broadcasted_iota(jnp.int32, parts.shape, 1)
    level = jnp.where(spot < GROUP, level, 0.0).reshape(CTXN, OWN, HEAD_DIM)
    factor = jnp.exp(level - jnp.max(level, axis=0, keepdims=True))
    factor = factor * (1.0 / jnp.sum(factor, axis=0, keepdims=True))
    joined = []
    for s in range(GROUP):
        total = jnp.zeros((OWN, HEAD_DIM), jnp.float32)
        for c in range(CTXN):
            outs = back_ref[c, :, s * HEAD_DIM : (s + 1) * HEAD_DIM].astype(jnp.float32)
            total = total + outs * factor[c, :, s : s + 1]
        joined.append(total.astype(jnp.bfloat16))
    attended = jnp.concatenate(joined, axis=1)
    for c in range(CTXN):
        rows_ref[c] = attended


def rotary_table(positions):
    half = HEAD_DIM // 2
    frequency = 500000.0 ** (-(jnp.arange(half, dtype=jnp.float32) * 2.0 / HEAD_DIM))
    angles = positions.astype(jnp.float32)[:, None] * frequency[None, :]
    cosine, sine = jnp.cos(angles), jnp.sin(angles)
    return jnp.concatenate([cosine, cosine, -sine, sine], axis=1)


def per_device(hidden, norm_gain, w_qkv, positions, cache_keys, cache_values, key_counts, w_out):
    bf16, f32 = jnp.bfloat16, jnp.float32
    y, z = lax.axis_index("y").astype(jnp.int32), lax.axis_index("z").astype(jnp.int32)
    head = lax.axis_index(HEAD).astype(jnp.int32)
    sent, own_columns = pl.pallas_call(
        split_kernel,
        in_specs=[SMEM, VMEM, VMEM, ANY],
        out_specs=[VMEM, VMEM],
        out_shape=[shape((YN * HN, OWN, 2 * HEAD_DIM), bf16), shape((HEAD_DIM, WIDTH), bf16)],
        scratch_shapes=[pltpu.SemaphoreType.DMA],
        name="split",
    )(head[None], hidden, norm_gain[None, :], w_qkv)
    columns = [own_columns] + [
        lax.ppermute(own_columns, "y", [(i, (i + k) % YN) for i in range(YN)]) for k in range(1, YN)
    ]
    got = exchange(sent, ("y", "x", "core"))
    first_own = z * (OWN * YN) + y * OWN
    info = jnp.stack([key_counts[0], first_own, y])
    table = rotary_table(lax.dynamic_slice_in_dim(positions, first_own, OWN))
    mix = pl.pallas_call(
        project_kernel,
        in_specs=[SMEM] + [VMEM] * 8,
        out_specs=VMEM,
        out_shape=shape((ZN, OWN, WIDTH + HEAD_DIM), f32),
        compiler_params=params(16),
        name="project",
    )(info, got, *columns, table, cache_keys, cache_values)
    mix = exchange(mix, "z")
    queries, new_rows = pl.pallas_call(
        turn_kernel,
        in_specs=[VMEM, VMEM],
        out_specs=[VMEM, VMEM],
        out_shape=[shape((CTXN, OWN, FLAT), bf16), shape((OWN, 2 * HEAD_DIM), bf16)],
        name="turn",
    )(mix, table)
    queries = exchange(queries, ("z", "y"))
    part = pl.pallas_call(
        attend_kernel,
        in_specs=[SMEM, VMEM, VMEM, VMEM, VMEM],
        out_specs=VMEM,
        out_shape=shape((CTXN, OWN, FLAT + HEAD_DIM), bf16),
        compiler_params=params(40),
        name="attend",
    )(info, queries, cache_keys, cache_values, new_rows)
    part = exchange(part, CTX)
    rows = pl.pallas_call(
        join_kernel,
        in_specs=[VMEM],
        out_specs=VMEM,
        out_shape=shape((CTXN, OWN, FLAT), bf16),
        name="join",
    )(part)
    rows = exchange(rows, CTX).reshape(TQ, FLAT)
    result = jnp.dot(rows, w_out, preferred_element_type=f32)
    result = exchange(result.reshape(HN, TQ // HN, HEAD_DIM), HEAD)
    return jnp.sum(result, axis=0).astype(bf16)


def solution(mesh):
    fine = Mesh(mesh.devices.reshape(YN, ZN, XN, CN), ("y", "z", "x", "core"))
    return jax.shard_map(
        per_device,
        mesh=fine,
        in_specs=(
            P(HEAD, CTX),
            P(CTX),
            P(CTX, None),
            P(),
            P(CTX, HEAD),
            P(CTX, HEAD),
            P(CTX),
            P(HEAD, CTX),
        ),
        out_specs=P(HEAD, CTX),
        check_vma=False,
    )
```

```python
import math

import jax
import jax.numpy as jnp
from jax import lax
from jax.experimental import pallas as pl
from jax.experimental.pallas import tpu as pltpu
from jax.sharding import Mesh
from jax.sharding import PartitionSpec as P

D = 4096
HEADS = 32
KV_HEADS = 8
HEAD_DIM = 128
GROUP = HEADS // KV_HEADS
SLOTS = GROUP + 2
WIDTH = SLOTS * HEAD_DIM
FLAT = GROUP * HEAD_DIM
TQ = 512
KEYS_DEV = 4096
NEG_FILL = -1e30
SCALE = 1.0 / math.sqrt(HEAD_DIM)
SCALE2 = SCALE * 1.4426950408889634

YN, ZN, XN, CN = 4, 8, 4, 2
HN = XN * CN
CTXN = YN * ZN
CTX = ("y", "z")
HEAD = ("x", "core")
OWN = TQ // CTXN
TAIL = 128
KEY_TILE = 512
PAIR = 2

VMEM = pl.BlockSpec(memory_space=pltpu.VMEM)
SMEM = pl.BlockSpec(memory_space=pltpu.SMEM)


def shape(dims, kind):
    return jax.ShapeDtypeStruct(dims, kind)


def params(mib=8):
    return pltpu.CompilerParams(vmem_limit_bytes=mib * 1024 * 1024)


def exchange(array, axes):
    return lax.all_to_all(array, axes, 0, 0, tiled=True)


def split_kernel(hidden_ref, gain_ref, sent_ref):
    hidden = hidden_ref[...]
    scaled = (hidden.astype(jnp.float32) * gain_ref[...]).astype(jnp.bfloat16)
    both = jnp.concatenate([hidden, scaled], axis=1)
    for y in range(YN):
        for h in range(HN):
            sent_ref[y * HN + h] = both[y * OWN : (y + 1) * OWN]


def project_kernel(info_ref, got_ref, w0, w1, w2, w3, table_ref, k_ref, mix_ref):
    y = info_ref[2]
    total = None
    square = None
    for shift, w in enumerate((w0, w1, w2, w3)):
        source = lax.rem(y + YN - shift, YN)
        part = got_ref[pl.ds(source * HN, HN)].reshape(HN * OWN, 2 * HEAD_DIM)
        term = jnp.dot(part[:, HEAD_DIM:], w[...], preferred_element_type=jnp.float32)
        plain = part[:, :HEAD_DIM].astype(jnp.float32)
        own = jnp.sum(plain * plain, axis=1, keepdims=True)
        total = term if total is None else total + term
        square = own if square is None else square + own
    mix_ref[:, :, :WIDTH] = total.reshape(ZN, OWN, WIDTH)
    mix_ref[:, :, WIDTH:] = jnp.broadcast_to(square, (HN * OWN, HEAD_DIM)).reshape(ZN, OWN, HEAD_DIM)


def turn_kernel(mix_ref, table_ref, queries_ref, new_ref):
    share = mix_ref[0]
    for z in range(1, ZN):
        share = share + mix_ref[z]
    inv_rms = lax.rsqrt(share[:, WIDTH : WIDTH + 1] / D + 1e-05)
    cosine, sine = table_ref[:, :HEAD_DIM], table_ref[:, HEAD_DIM:]
    slots = []
    for s in range(SLOTS):
        value = share[:, s * HEAD_DIM : (s + 1) * HEAD_DIM] * inv_rms
        if s <= GROUP:
            value = value * cosine + pltpu.roll(value, HEAD_DIM // 2, 1) * sine
        slots.append(value.astype(jnp.bfloat16))
    queries = jnp.concatenate(slots[:GROUP], axis=1)
    for c in range(CTXN):
        queries_ref[c] = queries
    new_ref[...] = jnp.concatenate(slots[GROUP:], axis=1)


def attend_kernel(info_ref, q_ref, k_ref, v_ref, new_ref, o_ref):
    count = info_ref[0]
    first_own = info_ref[1]
    rows = PAIR * TQ

    def lane(n):
        return lax.broadcasted_iota(jnp.int32, (n, HEAD_DIM), 1)

    def first_lane(n):
        return jnp.where(lane(n) == 0, 1.0, 0.0).astype(jnp.bfloat16)

    def product(a, b):
        return lax.dot_general(a, b, (((1,), (1,)), ((), ())), preferred_element_type=jnp.float32)

    asked = lax.broadcasted_iota(jnp.int32, (rows, TAIL), 0) % TQ
    own = lax.broadcasted_iota(jnp.int32, (rows, TAIL), 1)
    seen = (own < OWN) & (own + first_own <= asked)
    blank = jnp.zeros((TAIL - OWN, HEAD_DIM), jnp.bfloat16)
    tail_keys = jnp.concatenate([new_ref[:, :HEAD_DIM], blank], axis=0)
    tail_values = jnp.concatenate([new_ref[:, HEAD_DIM:], blank], axis=0)
    spot = lane(TQ)
    packed = jnp.zeros((TQ, HEAD_DIM), jnp.float32)
    for pair in range(GROUP // PAIR):
        slots = range(pair * PAIR, (pair + 1) * PAIR)
        queries = jnp.concatenate(
            [q_ref[:, :, s * HEAD_DIM : (s + 1) * HEAD_DIM].reshape(TQ, HEAD_DIM) for s in slots], axis=0
        )
        wide = jnp.concatenate([queries, first_lane(rows)], axis=1)
        best = jnp.full((rows, 1), NEG_FILL, jnp.float32)
        sums = jnp.zeros((rows, 2 * HEAD_DIM), jnp.float32)
        for start in range(0, KEYS_DEV + TAIL, KEY_TILE):
            if start < KEYS_DEV:
                index = lax.broadcasted_iota(jnp.int32, (KEY_TILE, HEAD_DIM), 0) + start
                hide = jnp.where((lane(KEY_TILE) == 0) & (index >= count), NEG_FILL, 0.0).astype(jnp.bfloat16)
                keys = jnp.concatenate([k_ref[start : start + KEY_TILE, :], hide], axis=1)
                values = jnp.concatenate([v_ref[start : start + KEY_TILE, :], first_lane(KEY_TILE)], axis=1)
                scores = product(wide, keys)
            else:
                values = jnp.concatenate([tail_values, first_lane(TAIL)], axis=1)
                scores = jnp.where(seen, product(queries, tail_keys), NEG_FILL)
            higher = jnp.maximum(best, jnp.max(scores, axis=1, keepdims=True))
            weights = jnp.exp2(scores * SCALE2 - higher * SCALE2).astype(jnp.bfloat16)
            sums = sums * jnp.exp2((best - higher) * SCALE2) + jnp.dot(
                weights, values, preferred_element_type=jnp.float32
            )
            best = higher
        total = sums[:, HEAD_DIM : HEAD_DIM + 1]
        outs = (sums[:, :HEAD_DIM] * (1.0 / total)).astype(jnp.bfloat16)
        level = best * SCALE + jnp.log(total)
        high = level.astype(jnp.bfloat16).astype(jnp.float32)
        mid = (level - high).astype(jnp.bfloat16).astype(jnp.float32)
        low = (level - high) - mid
        for n, s in enumerate(slots):
            here = slice(n * TQ, (n + 1) * TQ)
            o_ref[:, :, s * HEAD_DIM : (s + 1) * HEAD_DIM] = outs[here].reshape(CTXN, OWN, HEAD_DIM)
            for step, piece in enumerate((high, mid, low)):
                packed = jnp.where(spot == step * GROUP + s, piece[here], packed)
    o_ref[:, :, FLAT:] = packed.astype(jnp.bfloat16).reshape(CTXN, OWN, HEAD_DIM)


def join_kernel(back_ref, rows_ref):
    parts = back_ref[:, :, FLAT:].astype(jnp.float32).reshape(CTXN * OWN, HEAD_DIM)
    level = parts + pltpu.roll(parts, HEAD_DIM - GROUP, 1) + pltpu.roll(parts, HEAD_DIM - 2 * GROUP, 1)
    spot = lax.broadcasted_iota(jnp.int32, parts.shape, 1)
    level = jnp.where(spot < GROUP, level, 0.0).reshape(CTXN, OWN, HEAD_DIM)
    factor = jnp.exp(level - jnp.max(level, axis=0, keepdims=True))
    factor = factor * (1.0 / jnp.sum(factor, axis=0, keepdims=True))
    joined = []
    for s in range(GROUP):
        total = jnp.zeros((OWN, HEAD_DIM), jnp.float32)
        for c in range(CTXN):
            outs = back_ref[c, :, s * HEAD_DIM : (s + 1) * HEAD_DIM].astype(jnp.float32)
            total = total + outs * factor[c, :, s : s + 1]
        joined.append(total.astype(jnp.bfloat16))
    attended = jnp.concatenate(joined, axis=1)
    for c in range(CTXN):
        rows_ref[c] = attended


def rotary_table(positions):
    half = HEAD_DIM // 2
    frequency = 500000.0 ** (-(jnp.arange(half, dtype=jnp.float32) * 2.0 / HEAD_DIM))
    angles = positions.astype(jnp.float32)[:, None] * frequency[None, :]
    cosine, sine = jnp.cos(angles), jnp.sin(angles)
    return jnp.concatenate([cosine, cosine, -sine, sine], axis=1)


def per_device(hidden, norm_gain, w_qkv, positions, cache_keys, cache_values, key_counts, w_out):
    bf16, f32 = jnp.bfloat16, jnp.float32
    y, z = lax.axis_index("y").astype(jnp.int32), lax.axis_index("z").astype(jnp.int32)
    head = lax.axis_index(HEAD).astype(jnp.int32)
    own_columns = lax.dynamic_slice_in_dim(w_qkv, head * WIDTH, WIDTH, axis=1)
    sent = pl.pallas_call(
        split_kernel,
        in_specs=[VMEM, VMEM],
        out_specs=VMEM,
        out_shape=shape((YN * HN, OWN, 2 * HEAD_DIM), bf16),
        compiler_params=params(56),
        name="split",
    )(hidden, norm_gain[None, :])
    columns = [own_columns] + [
        lax.ppermute(own_columns, "y", [(i, (i + k) % YN) for i in range(YN)]) for k in range(1, YN)
    ]
    got = exchange(sent, ("y", "x", "core"))
    first_own = z * (OWN * YN) + y * OWN
    info = jnp.stack([key_counts[0], first_own, y])
    table = rotary_table(lax.dynamic_slice_in_dim(positions, first_own, OWN))
    mix = pl.pallas_call(
        project_kernel,
        in_specs=[SMEM] + [VMEM] * 7,
        out_specs=VMEM,
        out_shape=shape((ZN, OWN, WIDTH + HEAD_DIM), f32),
        compiler_params=params(16),
        name="project",
    )(info, got, *columns, table, cache_keys)
    mix = exchange(mix, "z")
    queries, new_rows = pl.pallas_call(
        turn_kernel,
        in_specs=[VMEM, VMEM],
        out_specs=[VMEM, VMEM],
        out_shape=[shape((CTXN, OWN, FLAT), bf16), shape((OWN, 2 * HEAD_DIM), bf16)],
        compiler_params=params(),
        name="turn",
    )(mix, table)
    queries = exchange(queries, ("z", "y"))
    part = pl.pallas_call(
        attend_kernel,
        in_specs=[SMEM, VMEM, VMEM, VMEM, VMEM],
        out_specs=VMEM,
        out_shape=shape((CTXN, OWN, FLAT + HEAD_DIM), bf16),
        compiler_params=params(40),
        name="attend",
    )(info, queries, cache_keys, cache_values, new_rows)
    part = exchange(part, CTX)
    rows = pl.pallas_call(
        join_kernel,
        in_specs=[VMEM],
        out_specs=VMEM,
        out_shape=shape((CTXN, OWN, FLAT), bf16),
        compiler_params=params(),
        name="join",
    )(part)
    rows = exchange(rows, CTX).reshape(TQ, FLAT)
    result = jnp.dot(rows, w_out, preferred_element_type=f32)
    result = exchange(result.reshape(HN, TQ // HN, HEAD_DIM), HEAD)
    return jnp.sum(result, axis=0).astype(bf16)


def solution(mesh):
    fine = Mesh(mesh.devices.reshape(YN, ZN, XN, CN), ("y", "z", "x", "core"))
    return jax.shard_map(
        per_device,
        mesh=fine,
        in_specs=(
            P(HEAD, CTX),
            P(CTX),
            P(CTX, None),
            P(),
            P(CTX, HEAD),
            P(CTX, HEAD),
            P(CTX),
            P(HEAD, CTX),
        ),
        out_specs=P(HEAD, CTX),
        check_vma=False,
    )
```

```python
import functools
import math

import jax
import jax.numpy as jnp
from jax import lax
from jax.experimental import pallas as pl
from jax.experimental.pallas import tpu as pltpu
from jax.sharding import Mesh
from jax.sharding import PartitionSpec as P

D = 4096
HEADS = 32
KV_HEADS = 8
HEAD_DIM = 128
GROUP = HEADS // KV_HEADS
SLOTS = GROUP + 2
WIDTH = SLOTS * HEAD_DIM
FLAT = GROUP * HEAD_DIM
TQ = 512
KEYS_DEV = 4096
NEG_FILL = -1e30
SCALE = 1.0 / math.sqrt(HEAD_DIM)
SCALE2 = SCALE * 1.4426950408889634

YN, ZN, XN, CN = 4, 8, 4, 2
HN = XN * CN
CTXN = YN * ZN
CTX = ("y", "z")
HEAD = ("x", "core")
OWN = TQ // CTXN
TAIL = 128
KEY_TILE = 512
SHARE = OWN * ZN

VMEM = pl.BlockSpec(memory_space=pltpu.VMEM)
SMEM = pl.BlockSpec(memory_space=pltpu.SMEM)


def shape(dims, kind):
    return jax.ShapeDtypeStruct(dims, kind)


def params(mib=8):
    return pltpu.CompilerParams(vmem_limit_bytes=mib * 1024 * 1024)


def exchange(array, axes):
    return lax.all_to_all(array, axes, 0, 0, tiled=True)


def along_y(array, shift):
    if shift == 0:
        return array
    return lax.ppermute(array, "y", [(i, (i + shift) % YN) for i in range(YN)])


def split_kernel(hidden_ref, gain_ref, sent_ref):
    hidden = hidden_ref[...]
    scaled = (hidden.astype(jnp.float32) * gain_ref[...]).astype(jnp.bfloat16)
    both = jnp.concatenate([hidden, scaled], axis=1)
    for y in range(YN):
        for h in range(HN):
            sent_ref[y * HN + h] = both[y * OWN : (y + 1) * OWN]


def project_kernel(info_ref, got_ref, w0, w1, w2, w3, table_ref, k_ref, mix_ref):
    y = info_ref[2]
    total = None
    square = None
    for shift, w in enumerate((w0, w1, w2, w3)):
        source = lax.rem(y + YN - shift, YN)
        part = got_ref[pl.ds(source * HN, HN)].reshape(HN * OWN, 2 * HEAD_DIM)
        term = jnp.dot(part[:, HEAD_DIM:], w[...], preferred_element_type=jnp.float32)
        plain = part[:, :HEAD_DIM].astype(jnp.float32)
        own = jnp.sum(plain * plain, axis=1, keepdims=True)
        total = term if total is None else total + term
        square = own if square is None else square + own
    mix_ref[:, :, :WIDTH] = total.reshape(ZN, OWN, WIDTH)
    mix_ref[:, :, WIDTH:] = jnp.broadcast_to(square, (HN * OWN, HEAD_DIM)).reshape(ZN, OWN, HEAD_DIM)


def turn_kernel(mix_ref, table_ref, queries_ref, new_ref):
    share = mix_ref[0]
    for z in range(1, ZN):
        share = share + mix_ref[z]
    inv_rms = lax.rsqrt(share[:, WIDTH : WIDTH + 1] / D + 1e-05)
    cosine, sine = table_ref[:, :HEAD_DIM], table_ref[:, HEAD_DIM:]
    slots = []
    for s in range(SLOTS):
        value = share[:, s * HEAD_DIM : (s + 1) * HEAD_DIM] * inv_rms
        if s <= GROUP:
            value = value * cosine + pltpu.roll(value, HEAD_DIM // 2, 1) * sine
        slots.append(value.astype(jnp.bfloat16))
    queries = jnp.concatenate(slots[:GROUP], axis=1)
    for z in range(ZN):
        queries_ref[z] = queries
    new_ref[...] = jnp.concatenate(slots[GROUP:], axis=1)


def packed_levels(level):
    high = level.astype(jnp.bfloat16).astype(jnp.float32)
    mid = (level - high).astype(jnp.bfloat16).astype(jnp.float32)
    low = (level - high) - mid
    return (high + pltpu.roll(mid, GROUP, 1) + pltpu.roll(low, 2 * GROUP, 1)).astype(jnp.bfloat16)


def levels_of(parts):
    parts = parts.astype(jnp.float32)
    level = parts + pltpu.roll(parts, HEAD_DIM - GROUP, 1) + pltpu.roll(parts, HEAD_DIM - 2 * GROUP, 1)
    spot = lax.broadcasted_iota(jnp.int32, parts.shape, 1)
    return jnp.where(spot < GROUP, level, 0.0)


def attend_kernel(shift, info_ref, q_ref, k_ref, v_ref, new_ref, o_ref):
    count = info_ref[0]
    first_own = info_ref[1]
    source = lax.rem(info_ref[2] + YN - shift, YN)
    rows = GROUP * SHARE

    def lane(n):
        return lax.broadcasted_iota(jnp.int32, (n, HEAD_DIM), 1)

    def first_lane(n):
        return jnp.where(lane(n) == 0, 1.0, 0.0).astype(jnp.bfloat16)

    def product(a, b):
        return lax.dot_general(a, b, (((1,), (1,)), ((), ())), preferred_element_type=jnp.float32)

    place = lax.broadcasted_iota(jnp.int32, (rows, TAIL), 0) % SHARE
    asked = (place // OWN) * (OWN * YN) + source * OWN + place % OWN
    own = lax.broadcasted_iota(jnp.int32, (rows, TAIL), 1)
    seen = (own < OWN) & (own + first_own <= asked)
    blank = jnp.zeros((TAIL - OWN, HEAD_DIM), jnp.bfloat16)
    tail_keys = jnp.concatenate([new_ref[:, :HEAD_DIM], blank], axis=0)
    tail_values = jnp.concatenate([new_ref[:, HEAD_DIM:], blank], axis=0)
    queries = jnp.concatenate(
        [q_ref[:, :, s * HEAD_DIM : (s + 1) * HEAD_DIM].reshape(SHARE, HEAD_DIM) for s in range(GROUP)], axis=0
    )
    wide = jnp.concatenate([queries, first_lane(rows)], axis=1)
    best = jnp.full((rows, 1), NEG_FILL, jnp.float32)
    sums = jnp.zeros((rows, 2 * HEAD_DIM), jnp.float32)
    for start in range(0, KEYS_DEV + TAIL, KEY_TILE):
        if start < KEYS_DEV:
            index = lax.broadcasted_iota(jnp.int32, (KEY_TILE, HEAD_DIM), 0) + start
            hide = jnp.where((lane(KEY_TILE) == 0) & (index >= count), NEG_FILL, 0.0).astype(jnp.bfloat16)
            keys = jnp.concatenate([k_ref[start : start + KEY_TILE, :], hide], axis=1)
            values = jnp.concatenate([v_ref[start : start + KEY_TILE, :], first_lane(KEY_TILE)], axis=1)
            scores = product(wide, keys)
        else:
            values = jnp.concatenate([tail_values, first_lane(TAIL)], axis=1)
            scores = jnp.where(seen, product(queries, tail_keys), NEG_FILL)
        higher = jnp.maximum(best, jnp.max(scores, axis=1, keepdims=True))
        weights = jnp.exp2(scores * SCALE2 - higher * SCALE2).astype(jnp.bfloat16)
        sums = sums * jnp.exp2((best - higher) * SCALE2) + jnp.dot(
            weights, values, preferred_element_type=jnp.float32
        )
        best = higher
    total = sums[:, HEAD_DIM : HEAD_DIM + 1]
    outs = (sums[:, :HEAD_DIM] * (1.0 / total)).astype(jnp.bfloat16)
    level = best * SCALE + jnp.log(total)
    spot = lane(SHARE)
    levels = jnp.zeros((SHARE, HEAD_DIM), jnp.float32)
    for s in range(GROUP):
        here = slice(s * SHARE, (s + 1) * SHARE)
        o_ref[:, :, s * HEAD_DIM : (s + 1) * HEAD_DIM] = outs[here].reshape(ZN, OWN, HEAD_DIM)
        levels = jnp.where(spot == s, level[here], levels)
    o_ref[:, :, FLAT:] = packed_levels(levels).reshape(ZN, OWN, HEAD_DIM)


def merge_kernel(own_ref, one_ref, two_ref, three_ref, w1, w2, w3, o_ref):
    refs = (own_ref, one_ref, two_ref, three_ref)
    levels = [levels_of(ref[:, :, FLAT:].reshape(SHARE, HEAD_DIM)) for ref in refs]
    most = levels[0]
    for level in levels[1:]:
        most = jnp.maximum(most, level)
    factors = [jnp.exp(level - most) for level in levels]
    total = factors[0] + factors[1] + factors[2] + factors[3]
    factors = [factor * (1.0 / total) for factor in factors]
    for s in range(GROUP):
        here = slice(s * HEAD_DIM, (s + 1) * HEAD_DIM)
        joined = jnp.zeros((SHARE, HEAD_DIM), jnp.float32)
        for ref, factor in zip(refs, factors):
            joined = joined + ref[:, :, here].reshape(SHARE, HEAD_DIM).astype(jnp.float32) * factor[:, s : s + 1]
        o_ref[:, :, here] = joined.astype(jnp.bfloat16).reshape(ZN, OWN, HEAD_DIM)
    spot = lax.broadcasted_iota(jnp.int32, most.shape, 1)
    level = jnp.where(spot < GROUP, most + jnp.log(total), 0.0)
    o_ref[:, :, FLAT:] = packed_levels(level).reshape(ZN, OWN, HEAD_DIM)


def join_kernel(back_ref, rows_ref):
    level = levels_of(back_ref[:, :, FLAT:].reshape(SHARE, HEAD_DIM)).reshape(ZN, OWN, HEAD_DIM)
    factor = jnp.exp(level - jnp.max(level, axis=0, keepdims=True))
    factor = factor * (1.0 / jnp.sum(factor, axis=0, keepdims=True))
    joined = []
    for s in range(GROUP):
        total = jnp.zeros((OWN, HEAD_DIM), jnp.float32)
        for z in range(ZN):
            outs = back_ref[z, :, s * HEAD_DIM : (s + 1) * HEAD_DIM].astype(jnp.float32)
            total = total + outs * factor[z, :, s : s + 1]
        joined.append(total.astype(jnp.bfloat16))
    attended = jnp.concatenate(joined, axis=1)
    for z in range(ZN):
        rows_ref[z] = attended


def finish_kernel(info_ref, rows_ref, w0, w1, w2, w3, o_ref):
    rows = rows_ref[...].reshape(SHARE, FLAT)
    for shift, w in enumerate((w0, w1, w2, w3)):
        source = lax.rem(info_ref[2] + YN - shift, YN)
        term = jnp.dot(rows, w[...], preferred_element_type=jnp.float32)
        o_ref[pl.ds(source * HN, HN)] = term.reshape(HN, OWN, HEAD_DIM)


def rotary_table(positions):
    half = HEAD_DIM // 2
    frequency = 500000.0 ** (-(jnp.arange(half, dtype=jnp.float32) * 2.0 / HEAD_DIM))
    angles = positions.astype(jnp.float32)[:, None] * frequency[None, :]
    cosine, sine = jnp.cos(angles), jnp.sin(angles)
    return jnp.concatenate([cosine, cosine, -sine, sine], axis=1)


def per_device(hidden, norm_gain, w_qkv, positions, cache_keys, cache_values, key_counts, w_out):
    bf16, f32 = jnp.bfloat16, jnp.float32
    y, z = lax.axis_index("y").astype(jnp.int32), lax.axis_index("z").astype(jnp.int32)
    head = lax.axis_index(HEAD).astype(jnp.int32)
    own_columns = lax.dynamic_slice_in_dim(w_qkv, head * WIDTH, WIDTH, axis=1)
    sent = pl.pallas_call(
        split_kernel,
        in_specs=[VMEM, VMEM],
        out_specs=VMEM,
        out_shape=shape((YN * HN, OWN, 2 * HEAD_DIM), bf16),
        compiler_params=params(56),
        name="split",
    )(hidden, norm_gain[None, :])
    columns = [along_y(own_columns, shift) for shift in range(YN)]
    got = exchange(sent, ("y", "x", "core"))
    first_own = z * (OWN * YN) + y * OWN
    info = jnp.stack([key_counts[0], first_own, y])
    table = rotary_table(lax.dynamic_slice_in_dim(positions, first_own, OWN))
    mix = pl.pallas_call(
        project_kernel,
        in_specs=[SMEM] + [VMEM] * 7,
        out_specs=VMEM,
        out_shape=shape((ZN, OWN, WIDTH + HEAD_DIM), f32),
        compiler_params=params(16),
        name="project",
    )(info, got, *columns, table, cache_keys)
    mix = exchange(mix, "z")
    queries, new_rows = pl.pallas_call(
        turn_kernel,
        in_specs=[VMEM, VMEM],
        out_specs=[VMEM, VMEM],
        out_shape=[shape((ZN, OWN, FLAT), bf16), shape((OWN, 2 * HEAD_DIM), bf16)],
        compiler_params=params(),
        name="turn",
    )(mix, table)
    queries = exchange(queries, "z")
    parts = []
    for shift in range(YN):
        part = pl.pallas_call(
            functools.partial(attend_kernel, shift),
            in_specs=[SMEM, VMEM, VMEM, VMEM, VMEM],
            out_specs=VMEM,
            out_shape=shape((ZN, OWN, FLAT + HEAD_DIM), bf16),
            compiler_params=params(24),
            cost_estimate=pl.CostEstimate(flops=4_000_000_000, bytes_accessed=0, transcendentals=0),
            name="attend",
        )(info, along_y(queries, shift), cache_keys, cache_values, new_rows)
        parts.append(along_y(part, -shift))
    w_outs = [along_y(w_out, shift) for shift in range(YN)]
    part = pl.pallas_call(
        merge_kernel,
        in_specs=[VMEM] * 7,
        out_specs=VMEM,
        out_shape=shape((ZN, OWN, FLAT + HEAD_DIM), bf16),
        compiler_params=params(),
        name="merge",
    )(*parts, *w_outs[1:])
    part = exchange(part, "z")
    rows = pl.pallas_call(
        join_kernel,
        in_specs=[VMEM],
        out_specs=VMEM,
        out_shape=shape((ZN, OWN, FLAT), bf16),
        compiler_params=params(),
        name="join",
    )(part)
    rows = exchange(rows, "z")
    result = pl.pallas_call(
        finish_kernel,
        in_specs=[SMEM] + [VMEM] * 5,
        out_specs=VMEM,
        out_shape=shape((YN * HN, OWN, HEAD_DIM), f32),
        compiler_params=params(),
        name="finish",
    )(info, rows, *w_outs)
    result = exchange(result, ("y", "x", "core")).reshape(YN, HN, OWN, HEAD_DIM)
    return jnp.sum(result, axis=1).reshape(YN * OWN, HEAD_DIM).astype(bf16)


def solution(mesh):
    fine = Mesh(mesh.devices.reshape(YN, ZN, XN, CN), ("y", "z", "x", "core"))
    return jax.shard_map(
        per_device,
        mesh=fine,
        in_specs=(
            P(HEAD, CTX),
            P(CTX),
            P(CTX, None),
            P(),
            P(CTX, HEAD),
            P(CTX, HEAD),
            P(CTX),
            P(HEAD, CTX),
        ),
        out_specs=P(HEAD, CTX),
        check_vma=False,
    )
```

```python
import functools
import math

import jax
import jax.numpy as jnp
from jax import lax
from jax.experimental import pallas as pl
from jax.experimental.pallas import tpu as pltpu
from jax.sharding import Mesh
from jax.sharding import PartitionSpec as P

D = 4096
HEADS = 32
KV_HEADS = 8
HEAD_DIM = 128
GROUP = HEADS // KV_HEADS
SLOTS = GROUP + 2
WIDTH = SLOTS * HEAD_DIM
FLAT = GROUP * HEAD_DIM
TQ = 512
KEYS_DEV = 4096
NEG_FILL = -1e30
SCALE = 1.0 / math.sqrt(HEAD_DIM)
SCALE2 = SCALE * 1.4426950408889634

YN, ZN, XN, CN = 4, 8, 4, 2
HN = XN * CN
CTXN = YN * ZN
CTX = ("y", "z")
HEAD = ("x", "core")
OWN = TQ // CTXN
TAIL = 128
KEY_TILE = 512
SHARE = OWN * ZN

VMEM = pl.BlockSpec(memory_space=pltpu.VMEM)
SMEM = pl.BlockSpec(memory_space=pltpu.SMEM)


def shape(dims, kind):
    return jax.ShapeDtypeStruct(dims, kind)


def params(mib=8):
    return pltpu.CompilerParams(vmem_limit_bytes=mib * 1024 * 1024)


def exchange(array, axes):
    return lax.all_to_all(array, axes, 0, 0, tiled=True)


def along_y(array, shift):
    if shift == 0:
        return array
    return lax.ppermute(array, "y", [(i, (i + shift) % YN) for i in range(YN)])


def split_kernel(hidden_ref, gain_ref, sent_ref):
    hidden = hidden_ref[...]
    scaled = (hidden.astype(jnp.float32) * gain_ref[...]).astype(jnp.bfloat16)
    both = jnp.concatenate([hidden, scaled], axis=1)
    for y in range(YN):
        for h in range(HN):
            sent_ref[y * HN + h] = both[y * OWN : (y + 1) * OWN]


def project_kernel(info_ref, got_ref, w0, w1, w2, w3, table_ref, k_ref, o1, o2, o3, mix_ref):
    y = info_ref[2]
    total = None
    square = None
    for shift, w in enumerate((w0, w1, w2, w3)):
        source = lax.rem(y + YN - shift, YN)
        part = got_ref[pl.ds(source * HN, HN)].reshape(HN * OWN, 2 * HEAD_DIM)
        term = jnp.dot(part[:, HEAD_DIM:], w[...], preferred_element_type=jnp.float32)
        plain = part[:, :HEAD_DIM].astype(jnp.float32)
        own = jnp.sum(plain * plain, axis=1, keepdims=True)
        total = term if total is None else total + term
        square = own if square is None else square + own
    mix_ref[:, :, :WIDTH] = total.reshape(ZN, OWN, WIDTH)
    mix_ref[:, :, WIDTH:] = jnp.broadcast_to(square, (HN * OWN, HEAD_DIM)).reshape(ZN, OWN, HEAD_DIM)


def turn_kernel(mix_ref, table_ref, queries_ref, new_ref):
    share = mix_ref[0]
    for z in range(1, ZN):
        share = share + mix_ref[z]
    inv_rms = lax.rsqrt(share[:, WIDTH : WIDTH + 1] / D + 1e-05)
    cosine, sine = table_ref[:, :HEAD_DIM], table_ref[:, HEAD_DIM:]
    slots = []
    for s in range(SLOTS):
        value = share[:, s * HEAD_DIM : (s + 1) * HEAD_DIM] * inv_rms
        if s <= GROUP:
            value = value * cosine + pltpu.roll(value, HEAD_DIM // 2, 1) * sine
        slots.append(value.astype(jnp.bfloat16))
    queries = jnp.concatenate(slots[:GROUP], axis=1)
    for z in range(ZN):
        queries_ref[z] = queries
    new_ref[...] = jnp.concatenate(slots[GROUP:], axis=1)


def packed_levels(level):
    high = level.astype(jnp.bfloat16).astype(jnp.float32)
    mid = (level - high).astype(jnp.bfloat16).astype(jnp.float32)
    low = (level - high) - mid
    return (high + pltpu.roll(mid, GROUP, 1) + pltpu.roll(low, 2 * GROUP, 1)).astype(jnp.bfloat16)


def levels_of(parts):
    parts = parts.astype(jnp.float32)
    level = parts + pltpu.roll(parts, HEAD_DIM - GROUP, 1) + pltpu.roll(parts, HEAD_DIM - 2 * GROUP, 1)
    spot = lax.broadcasted_iota(jnp.int32, parts.shape, 1)
    return jnp.where(spot < GROUP, level, 0.0)


def attend_kernel(shift, info_ref, q_ref, k_ref, v_ref, new_ref, o_ref):
    count = info_ref[0]
    first_own = info_ref[1]
    source = lax.rem(info_ref[2] + YN - shift, YN)
    rows = GROUP * SHARE

    def lane(n):
        return lax.broadcasted_iota(jnp.int32, (n, HEAD_DIM), 1)

    def first_lane(n):
        return jnp.where(lane(n) == 0, 1.0, 0.0).astype(jnp.bfloat16)

    def product(a, b):
        return lax.dot_general(a, b, (((1,), (1,)), ((), ())), preferred_element_type=jnp.float32)

    place = lax.broadcasted_iota(jnp.int32, (rows, TAIL), 0) % SHARE
    asked = (place // OWN) * (OWN * YN) + source * OWN + place % OWN
    own = lax.broadcasted_iota(jnp.int32, (rows, TAIL), 1)
    seen = (own < OWN) & (own + first_own <= asked)
    blank = jnp.zeros((TAIL - OWN, HEAD_DIM), jnp.bfloat16)
    tail_keys = jnp.concatenate([new_ref[:, :HEAD_DIM], blank], axis=0)
    tail_values = jnp.concatenate([new_ref[:, HEAD_DIM:], blank], axis=0)
    queries = jnp.concatenate(
        [q_ref[:, :, s * HEAD_DIM : (s + 1) * HEAD_DIM].reshape(SHARE, HEAD_DIM) for s in range(GROUP)], axis=0
    )
    wide = jnp.concatenate([queries, first_lane(rows)], axis=1)
    best = jnp.full((rows, 1), NEG_FILL, jnp.float32)
    sums = jnp.zeros((rows, 2 * HEAD_DIM), jnp.float32)
    for start in range(0, KEYS_DEV + TAIL, KEY_TILE):
        if start < KEYS_DEV:
            index = lax.broadcasted_iota(jnp.int32, (KEY_TILE, HEAD_DIM), 0) + start
            hide = jnp.where((lane(KEY_TILE) == 0) & (index >= count), NEG_FILL, 0.0).astype(jnp.bfloat16)
            keys = jnp.concatenate([k_ref[start : start + KEY_TILE, :], hide], axis=1)
            values = jnp.concatenate([v_ref[start : start + KEY_TILE, :], first_lane(KEY_TILE)], axis=1)
            scores = product(wide, keys)
        else:
            values = jnp.concatenate([tail_values, first_lane(TAIL)], axis=1)
            scores = jnp.where(seen, product(queries, tail_keys), NEG_FILL)
        higher = jnp.maximum(best, jnp.max(scores, axis=1, keepdims=True))
        weights = jnp.exp2((scores - higher) * SCALE2).astype(jnp.bfloat16)
        sums = sums * jnp.exp2((best - higher) * SCALE2) + jnp.dot(
            weights, values, preferred_element_type=jnp.float32
        )
        best = higher
    total = sums[:, HEAD_DIM : HEAD_DIM + 1]
    outs = (sums[:, :HEAD_DIM] * (1.0 / total)).astype(jnp.bfloat16)
    level = best * SCALE + jnp.log(total)
    spot = lane(SHARE)
    levels = jnp.zeros((SHARE, HEAD_DIM), jnp.float32)
    for s in range(GROUP):
        here = slice(s * SHARE, (s + 1) * SHARE)
        o_ref[:, :, s * HEAD_DIM : (s + 1) * HEAD_DIM] = outs[here].reshape(ZN, OWN, HEAD_DIM)
        levels = jnp.where(spot == s, level[here], levels)
    o_ref[:, :, FLAT:] = packed_levels(levels).reshape(ZN, OWN, HEAD_DIM)


def merge_kernel(own_ref, one_ref, two_ref, three_ref, o_ref):
    refs = (own_ref, one_ref, two_ref, three_ref)
    levels = [levels_of(ref[:, :, FLAT:].reshape(SHARE, HEAD_DIM)) for ref in refs]
    most = levels[0]
    for level in levels[1:]:
        most = jnp.maximum(most, level)
    factors = [jnp.exp(level - most) for level in levels]
    total = factors[0] + factors[1] + factors[2] + factors[3]
    factors = [factor * (1.0 / total) for factor in factors]
    for s in range(GROUP):
        here = slice(s * HEAD_DIM, (s + 1) * HEAD_DIM)
        joined = jnp.zeros((SHARE, HEAD_DIM), jnp.float32)
        for ref, factor in zip(refs, factors):
            joined = joined + ref[:, :, here].reshape(SHARE, HEAD_DIM).astype(jnp.float32) * factor[:, s : s + 1]
        o_ref[:, :, here] = joined.astype(jnp.bfloat16).reshape(ZN, OWN, HEAD_DIM)
    spot = lax.broadcasted_iota(jnp.int32, most.shape, 1)
    level = jnp.where(spot < GROUP, most + jnp.log(total), 0.0)
    o_ref[:, :, FLAT:] = packed_levels(level).reshape(ZN, OWN, HEAD_DIM)


def join_kernel(back_ref, rows_ref):
    level = levels_of(back_ref[:, :, FLAT:].reshape(SHARE, HEAD_DIM)).reshape(ZN, OWN, HEAD_DIM)
    factor = jnp.exp(level - jnp.max(level, axis=0, keepdims=True))
    factor = factor * (1.0 / jnp.sum(factor, axis=0, keepdims=True))
    joined = []
    for s in range(GROUP):
        total = jnp.zeros((OWN, HEAD_DIM), jnp.float32)
        for z in range(ZN):
            outs = back_ref[z, :, s * HEAD_DIM : (s + 1) * HEAD_DIM].astype(jnp.float32)
            total = total + outs * factor[z, :, s : s + 1]
        joined.append(total.astype(jnp.bfloat16))
    attended = jnp.concatenate(joined, axis=1)
    for z in range(ZN):
        rows_ref[z] = attended


def finish_kernel(info_ref, rows_ref, w0, w1, w2, w3, o_ref):
    rows = rows_ref[...].reshape(SHARE, FLAT)
    for shift, w in enumerate((w0, w1, w2, w3)):
        source = lax.rem(info_ref[2] + YN - shift, YN)
        term = jnp.dot(rows, w[...], preferred_element_type=jnp.float32)
        o_ref[pl.ds(source * HN, HN)] = term.reshape(HN, OWN, HEAD_DIM)


def rotary_table(positions):
    half = HEAD_DIM // 2
    frequency = 500000.0 ** (-(jnp.arange(half, dtype=jnp.float32) * 2.0 / HEAD_DIM))
    angles = positions.astype(jnp.float32)[:, None] * frequency[None, :]
    cosine, sine = jnp.cos(angles), jnp.sin(angles)
    return jnp.concatenate([cosine, cosine, -sine, sine], axis=1)


def per_device(hidden, norm_gain, w_qkv, positions, cache_keys, cache_values, key_counts, w_out):
    bf16, f32 = jnp.bfloat16, jnp.float32
    y, z = lax.axis_index("y").astype(jnp.int32), lax.axis_index("z").astype(jnp.int32)
    head = lax.axis_index(HEAD).astype(jnp.int32)
    own_columns = lax.dynamic_slice_in_dim(w_qkv, head * WIDTH, WIDTH, axis=1)
    sent = pl.pallas_call(
        split_kernel,
        in_specs=[VMEM, VMEM],
        out_specs=VMEM,
        out_shape=shape((YN * HN, OWN, 2 * HEAD_DIM), bf16),
        compiler_params=params(56),
        name="split",
    )(hidden, norm_gain[None, :])
    w_outs = [along_y(w_out, shift) for shift in range(YN)]
    columns = [along_y(own_columns, shift) for shift in range(YN)]
    got = exchange(sent, ("y", "x", "core"))
    first_own = z * (OWN * YN) + y * OWN
    info = jnp.stack([key_counts[0], first_own, y])
    table = rotary_table(lax.dynamic_slice_in_dim(positions, first_own, OWN))
    mix = pl.pallas_call(
        project_kernel,
        in_specs=[SMEM] + [VMEM] * 10,
        out_specs=VMEM,
        out_shape=shape((ZN, OWN, WIDTH + HEAD_DIM), f32),
        compiler_params=params(16),
        name="project",
    )(info, got, *columns, table, cache_keys, *w_outs[1:])
    mix = exchange(mix, "z")
    queries, new_rows = pl.pallas_call(
        turn_kernel,
        in_specs=[VMEM, VMEM],
        out_specs=[VMEM, VMEM],
        out_shape=[shape((ZN, OWN, FLAT), bf16), shape((OWN, 2 * HEAD_DIM), bf16)],
        compiler_params=params(),
        name="turn",
    )(mix, table)
    queries = exchange(queries, "z")
    parts = []
    for shift in range(YN):
        part = pl.pallas_call(
            functools.partial(attend_kernel, shift),
            in_specs=[SMEM, VMEM, VMEM, VMEM, VMEM],
            out_specs=VMEM,
            out_shape=shape((ZN, OWN, FLAT + HEAD_DIM), bf16),
            compiler_params=params(24),
            cost_estimate=pl.CostEstimate(flops=4_000_000_000, bytes_accessed=0, transcendentals=0),
            name="attend",
        )(info, along_y(queries, shift), cache_keys, cache_values, new_rows)
        parts.append(along_y(part, -shift))
    part = pl.pallas_call(
        merge_kernel,
        in_specs=[VMEM] * 4,
        out_specs=VMEM,
        out_shape=shape((ZN, OWN, FLAT + HEAD_DIM), bf16),
        compiler_params=params(),
        name="merge",
    )(*parts)
    part = exchange(part, "z")
    rows = pl.pallas_call(
        join_kernel,
        in_specs=[VMEM],
        out_specs=VMEM,
        out_shape=shape((ZN, OWN, FLAT), bf16),
        compiler_params=params(),
        name="join",
    )(part)
    rows = exchange(rows, "z")
    result = pl.pallas_call(
        finish_kernel,
        in_specs=[SMEM] + [VMEM] * 5,
        out_specs=VMEM,
        out_shape=shape((YN * HN, OWN, HEAD_DIM), f32),
        compiler_params=params(),
        name="finish",
    )(info, rows, *w_outs)
    result = exchange(result, ("y", "x", "core")).reshape(YN, HN, OWN, HEAD_DIM)
    return jnp.sum(result, axis=1).reshape(YN * OWN, HEAD_DIM).astype(bf16)


def solution(mesh):
    fine = Mesh(mesh.devices.reshape(YN, ZN, XN, CN), ("y", "z", "x", "core"))
    return jax.shard_map(
        per_device,
        mesh=fine,
        in_specs=(
            P(HEAD, CTX),
            P(CTX),
            P(CTX, None),
            P(),
            P(CTX, HEAD),
            P(CTX, HEAD),
            P(CTX),
            P(HEAD, CTX),
        ),
        out_specs=P(HEAD, CTX),
        check_vma=False,
    )
```

```python
import functools
import math

import jax
import jax.numpy as jnp
from jax import lax
from jax.experimental import pallas as pl
from jax.experimental.pallas import tpu as pltpu
from jax.sharding import Mesh
from jax.sharding import PartitionSpec as P

D = 4096
HEADS = 32
KV_HEADS = 8
HEAD_DIM = 128
GROUP = HEADS // KV_HEADS
SLOTS = GROUP + 2
WIDTH = SLOTS * HEAD_DIM
FLAT = GROUP * HEAD_DIM
TQ = 512
KEYS_DEV = 4096
NEG_FILL = -1e30
SCALE = 1.0 / math.sqrt(HEAD_DIM)
SCALE2 = SCALE * 1.4426950408889634

YN, ZN, XN, CN = 4, 8, 4, 2
HN = XN * CN
CTXN = YN * ZN
CTX = ("y", "z")
HEAD = ("x", "core")
OWN = TQ // CTXN
TAIL = 128
KEY_TILE = 512
SHARE = OWN * ZN

VMEM = pl.BlockSpec(memory_space=pltpu.VMEM)
SMEM = pl.BlockSpec(memory_space=pltpu.SMEM)


def shape(dims, kind):
    return jax.ShapeDtypeStruct(dims, kind)


def params(mib=8):
    return pltpu.CompilerParams(vmem_limit_bytes=mib * 1024 * 1024)


def exchange(array, axes):
    return lax.all_to_all(array, axes, 0, 0, tiled=True)


def along_y(array, shift):
    if shift == 0:
        return array
    return lax.ppermute(array, "y", [(i, (i + shift) % YN) for i in range(YN)])


def split_kernel(hidden_ref, gain_ref, sent_ref):
    hidden = hidden_ref[...]
    scaled = (hidden.astype(jnp.float32) * gain_ref[...]).astype(jnp.bfloat16)
    both = jnp.concatenate([hidden, scaled], axis=1)
    for y in range(YN):
        for h in range(HN):
            sent_ref[y * HN + h] = both[y * OWN : (y + 1) * OWN]


def project_kernel(info_ref, got_ref, w0, w1, w2, w3, table_ref, k_ref, o1, o2, mix_ref):
    y = info_ref[2]
    total = None
    square = None
    for shift, w in enumerate((w0, w1, w2, w3)):
        source = lax.rem(y + YN - shift, YN)
        part = got_ref[pl.ds(source * HN, HN)].reshape(HN * OWN, 2 * HEAD_DIM)
        term = jnp.dot(part[:, HEAD_DIM:], w[...], preferred_element_type=jnp.float32)
        plain = part[:, :HEAD_DIM].astype(jnp.float32)
        own = jnp.sum(plain * plain, axis=1, keepdims=True)
        total = term if total is None else total + term
        square = own if square is None else square + own
    for s in range(SLOTS):
        part = total[:, s * HEAD_DIM : (s + 1) * HEAD_DIM]
        mix_ref[:, s * OWN : (s + 1) * OWN] = part.reshape(ZN, OWN, HEAD_DIM)
    wide = jnp.broadcast_to(square, (HN * OWN, HEAD_DIM)).reshape(ZN, OWN, HEAD_DIM)
    lane = lax.broadcasted_iota(jnp.int32, (ZN, OWN // 2, HEAD_DIM), 2)
    mix_ref[:, SLOTS * OWN :] = jnp.where(lane < HEAD_DIM // 2, wide[:, : OWN // 2], wide[:, OWN // 2 :])


def turn_kernel(mix_ref, table_ref, queries_ref, new_ref):
    share = mix_ref[0]
    for z in range(1, ZN):
        share = share + mix_ref[z]
    square = share[SLOTS * OWN :]
    half = HEAD_DIM // 2
    inv_rms = lax.rsqrt(jnp.concatenate([square[:, :1], square[:, half : half + 1]], axis=0) / D + 1e-05)
    cosine, sine = table_ref[:, :HEAD_DIM], table_ref[:, HEAD_DIM:]
    slots = []
    for s in range(SLOTS):
        value = share[s * OWN : (s + 1) * OWN] * inv_rms
        if s <= GROUP:
            value = value * cosine + pltpu.roll(value, HEAD_DIM // 2, 1) * sine
        slots.append(value.astype(jnp.bfloat16))
    queries = jnp.concatenate(slots[:GROUP], axis=1)
    for z in range(ZN):
        queries_ref[z] = queries
    new_ref[...] = jnp.concatenate(slots[GROUP:], axis=1)


def packed_levels(level):
    high = level.astype(jnp.bfloat16).astype(jnp.float32)
    mid = (level - high).astype(jnp.bfloat16).astype(jnp.float32)
    low = (level - high) - mid
    return (high + pltpu.roll(mid, GROUP, 1) + pltpu.roll(low, 2 * GROUP, 1)).astype(jnp.bfloat16)


def levels_of(parts):
    parts = parts.astype(jnp.float32)
    level = parts + pltpu.roll(parts, HEAD_DIM - GROUP, 1) + pltpu.roll(parts, HEAD_DIM - 2 * GROUP, 1)
    spot = lax.broadcasted_iota(jnp.int32, parts.shape, 1)
    return jnp.where(spot < GROUP, level, 0.0)


def attend_kernel(shift, info_ref, q_ref, k_ref, v_ref, new_ref, o_ref):
    count = info_ref[0]
    first_own = info_ref[1]
    source = lax.rem(info_ref[2] + YN - shift, YN)
    rows = GROUP * SHARE

    def lane(n):
        return lax.broadcasted_iota(jnp.int32, (n, HEAD_DIM), 1)

    def first_lane(n):
        return jnp.where(lane(n) == 0, 1.0, 0.0).astype(jnp.bfloat16)

    def product(a, b):
        return lax.dot_general(a, b, (((1,), (1,)), ((), ())), preferred_element_type=jnp.float32)

    place = lax.broadcasted_iota(jnp.int32, (rows, TAIL), 0) % SHARE
    asked = (place // OWN) * (OWN * YN) + source * OWN + place % OWN
    own = lax.broadcasted_iota(jnp.int32, (rows, TAIL), 1)
    seen = (own < OWN) & (own + first_own <= asked)
    blank = jnp.zeros((TAIL - OWN, HEAD_DIM), jnp.bfloat16)
    tail_keys = jnp.concatenate([new_ref[:, :HEAD_DIM], blank], axis=0)
    tail_values = jnp.concatenate([new_ref[:, HEAD_DIM:], blank], axis=0)
    queries = jnp.concatenate(
        [q_ref[:, :, s * HEAD_DIM : (s + 1) * HEAD_DIM].reshape(SHARE, HEAD_DIM) for s in range(GROUP)], axis=0
    )
    wide = jnp.concatenate([queries, first_lane(rows)], axis=1)
    best = jnp.full((rows, 1), NEG_FILL, jnp.float32)
    sums = jnp.zeros((rows, 2 * HEAD_DIM), jnp.float32)
    for start in range(0, KEYS_DEV + TAIL, KEY_TILE):
        if start < KEYS_DEV:
            index = lax.broadcasted_iota(jnp.int32, (KEY_TILE, HEAD_DIM), 0) + start
            hide = jnp.where((lane(KEY_TILE) == 0) & (index >= count), NEG_FILL, 0.0).astype(jnp.bfloat16)
            keys = jnp.concatenate([k_ref[start : start + KEY_TILE, :], hide], axis=1)
            values = jnp.concatenate([v_ref[start : start + KEY_TILE, :], first_lane(KEY_TILE)], axis=1)
            scores = product(wide, keys)
        else:
            values = jnp.concatenate([tail_values, first_lane(TAIL)], axis=1)
            scores = jnp.where(seen, product(queries, tail_keys), NEG_FILL)
        higher = jnp.maximum(best, jnp.max(scores, axis=1, keepdims=True))
        weights = jnp.exp2((scores - higher) * SCALE2).astype(jnp.bfloat16)
        sums = sums * jnp.exp2((best - higher) * SCALE2) + jnp.dot(
            weights, values, preferred_element_type=jnp.float32
        )
        best = higher
    total = sums[:, HEAD_DIM : HEAD_DIM + 1]
    outs = (sums[:, :HEAD_DIM] * (1.0 / total)).astype(jnp.bfloat16)
    level = best * SCALE + jnp.log(total)
    spot = lane(SHARE)
    levels = jnp.zeros((SHARE, HEAD_DIM), jnp.float32)
    for s in range(GROUP):
        here = slice(s * SHARE, (s + 1) * SHARE)
        o_ref[:, :, s * HEAD_DIM : (s + 1) * HEAD_DIM] = outs[here].reshape(ZN, OWN, HEAD_DIM)
        levels = jnp.where(spot == s, level[here], levels)
    o_ref[:, :, FLAT:] = packed_levels(levels).reshape(ZN, OWN, HEAD_DIM)


def merge_kernel(own_ref, one_ref, two_ref, three_ref, held_ref, o_ref):
    refs = (own_ref, one_ref, two_ref, three_ref)
    levels = [levels_of(ref[:, :, FLAT:].reshape(SHARE, HEAD_DIM)) for ref in refs]
    most = levels[0]
    for level in levels[1:]:
        most = jnp.maximum(most, level)
    factors = [jnp.exp(level - most) for level in levels]
    total = factors[0] + factors[1] + factors[2] + factors[3]
    factors = [factor * (1.0 / total) for factor in factors]
    for s in range(GROUP):
        here = slice(s * HEAD_DIM, (s + 1) * HEAD_DIM)
        joined = jnp.zeros((SHARE, HEAD_DIM), jnp.float32)
        for ref, factor in zip(refs, factors):
            joined = joined + ref[:, :, here].reshape(SHARE, HEAD_DIM).astype(jnp.float32) * factor[:, s : s + 1]
        o_ref[:, :, here] = joined.astype(jnp.bfloat16).reshape(ZN, OWN, HEAD_DIM)
    spot = lax.broadcasted_iota(jnp.int32, most.shape, 1)
    level = jnp.where(spot < GROUP, most + jnp.log(total), 0.0)
    o_ref[:, :, FLAT:] = packed_levels(level).reshape(ZN, OWN, HEAD_DIM)


def join_kernel(back_ref, rows_ref):
    level = levels_of(back_ref[:, :, FLAT:].reshape(SHARE, HEAD_DIM)).reshape(ZN, OWN, HEAD_DIM)
    factor = jnp.exp(level - jnp.max(level, axis=0, keepdims=True))
    factor = factor * (1.0 / jnp.sum(factor, axis=0, keepdims=True))
    joined = []
    for s in range(GROUP):
        total = jnp.zeros((OWN, HEAD_DIM), jnp.float32)
        for z in range(ZN):
            outs = back_ref[z, :, s * HEAD_DIM : (s + 1) * HEAD_DIM].astype(jnp.float32)
            total = total + outs * factor[z, :, s : s + 1]
        joined.append(total.astype(jnp.bfloat16))
    attended = jnp.concatenate(joined, axis=1)
    for z in range(ZN):
        rows_ref[z] = attended


def finish_kernel(info_ref, rows_ref, w0, w1, w2, w3, o_ref):
    rows = rows_ref[...].reshape(SHARE, FLAT)
    for shift, w in enumerate((w0, w1, w2, w3)):
        source = lax.rem(info_ref[2] + YN - shift, YN)
        term = jnp.dot(rows, w[...], preferred_element_type=jnp.float32)
        o_ref[pl.ds(source * HN, HN)] = term.reshape(HN, OWN, HEAD_DIM)


def rotary_table(positions):
    half = HEAD_DIM // 2
    frequency = 500000.0 ** (-(jnp.arange(half, dtype=jnp.float32) * 2.0 / HEAD_DIM))
    angles = positions.astype(jnp.float32)[:, None] * frequency[None, :]
    cosine, sine = jnp.cos(angles), jnp.sin(angles)
    return jnp.concatenate([cosine, cosine, -sine, sine], axis=1)


def per_device(hidden, norm_gain, w_qkv, positions, cache_keys, cache_values, key_counts, w_out):
    bf16, f32 = jnp.bfloat16, jnp.float32
    y, z = lax.axis_index("y").astype(jnp.int32), lax.axis_index("z").astype(jnp.int32)
    head = lax.axis_index(HEAD).astype(jnp.int32)
    own_columns = lax.dynamic_slice_in_dim(w_qkv, head * WIDTH, WIDTH, axis=1)
    sent = pl.pallas_call(
        split_kernel,
        in_specs=[VMEM, VMEM],
        out_specs=VMEM,
        out_shape=shape((YN * HN, OWN, 2 * HEAD_DIM), bf16),
        compiler_params=params(56),
        name="split",
    )(hidden, norm_gain[None, :])
    w_outs = [along_y(w_out, shift) for shift in range(YN)]
    columns = [along_y(own_columns, shift) for shift in range(YN)]
    got = exchange(sent, ("y", "x", "core"))
    first_own = z * (OWN * YN) + y * OWN
    info = jnp.stack([key_counts[0], first_own, y])
    table = rotary_table(lax.dynamic_slice_in_dim(positions, first_own, OWN))
    mix = pl.pallas_call(
        project_kernel,
        in_specs=[SMEM] + [VMEM] * 9,
        out_specs=VMEM,
        out_shape=shape((ZN, SLOTS * OWN + OWN // 2, HEAD_DIM), f32),
        compiler_params=params(16),
        name="project",
    )(info, got, *columns, table, cache_keys, w_outs[1], w_outs[3])
    mix = exchange(mix, "z")
    queries, new_rows = pl.pallas_call(
        turn_kernel,
        in_specs=[VMEM, VMEM],
        out_specs=[VMEM, VMEM],
        out_shape=[shape((ZN, OWN, FLAT), bf16), shape((OWN, 2 * HEAD_DIM), bf16)],
        compiler_params=params(),
        name="turn",
    )(mix, table)
    queries = exchange(queries, "z")
    parts = []
    for shift in range(YN):
        part = pl.pallas_call(
            functools.partial(attend_kernel, shift),
            in_specs=[SMEM, VMEM, VMEM, VMEM, VMEM],
            out_specs=VMEM,
            out_shape=shape((ZN, OWN, FLAT + HEAD_DIM), bf16),
            compiler_params=params(24),
            cost_estimate=pl.CostEstimate(flops=4_000_000_000, bytes_accessed=0, transcendentals=0),
            name="attend",
        )(info, along_y(queries, shift), cache_keys, cache_values, new_rows)
        parts.append(along_y(part, -shift))
    part = pl.pallas_call(
        merge_kernel,
        in_specs=[VMEM] * 5,
        out_specs=VMEM,
        out_shape=shape((ZN, OWN, FLAT + HEAD_DIM), bf16),
        compiler_params=params(),
        name="merge",
    )(*parts, w_outs[2])
    part = exchange(part, "z")
    rows = pl.pallas_call(
        join_kernel,
        in_specs=[VMEM],
        out_specs=VMEM,
        out_shape=shape((ZN, OWN, FLAT), bf16),
        compiler_params=params(),
        name="join",
    )(part)
    rows = exchange(rows, "z")
    result = pl.pallas_call(
        finish_kernel,
        in_specs=[SMEM] + [VMEM] * 5,
        out_specs=VMEM,
        out_shape=shape((YN * HN, OWN, HEAD_DIM), f32),
        compiler_params=params(),
        name="finish",
    )(info, rows, *w_outs)
    result = exchange(result, ("y", "x", "core")).reshape(YN, HN, OWN, HEAD_DIM)
    return jnp.sum(result, axis=1).reshape(YN * OWN, HEAD_DIM).astype(bf16)


def solution(mesh):
    fine = Mesh(mesh.devices.reshape(YN, ZN, XN, CN), ("y", "z", "x", "core"))
    return jax.shard_map(
        per_device,
        mesh=fine,
        in_specs=(
            P(HEAD, CTX),
            P(CTX),
            P(CTX, None),
            P(),
            P(CTX, HEAD),
            P(CTX, HEAD),
            P(CTX),
            P(HEAD, CTX),
        ),
        out_specs=P(HEAD, CTX),
        check_vma=False,
    )
```

```python
import functools
import math

import jax
import jax.numpy as jnp
from jax import lax
from jax.experimental import pallas as pl
from jax.experimental.pallas import tpu as pltpu
from jax.sharding import Mesh
from jax.sharding import PartitionSpec as P

D = 4096
HEADS = 32
KV_HEADS = 8
HEAD_DIM = 128
GROUP = HEADS // KV_HEADS
SLOTS = GROUP + 2
WIDTH = SLOTS * HEAD_DIM
FLAT = GROUP * HEAD_DIM
TQ = 512
KEYS_DEV = 4096
NEG_FILL = -1e30
SCALE = 1.0 / math.sqrt(HEAD_DIM)
SCALE2 = SCALE * 1.4426950408889634

YN, ZN, XN, CN = 4, 8, 4, 2
HN = XN * CN
CTXN = YN * ZN
CTX = ("y", "z")
HEAD = ("x", "core")
OWN = TQ // CTXN
TAIL = 128
KEY_TILE = 512
SHARE = OWN * ZN

VMEM = pl.BlockSpec(memory_space=pltpu.VMEM)
SMEM = pl.BlockSpec(memory_space=pltpu.SMEM)


def shape(dims, kind):
    return jax.ShapeDtypeStruct(dims, kind)


def params(mib=8):
    return pltpu.CompilerParams(vmem_limit_bytes=mib * 1024 * 1024)


def exchange(array, axes):
    return lax.all_to_all(array, axes, 0, 0, tiled=True)


def along_y(array, shift):
    if shift == 0:
        return array
    return lax.ppermute(array, "y", [(i, (i + shift) % YN) for i in range(YN)])


def split_kernel(hidden_ref, gain_ref, sent_ref):
    hidden = hidden_ref[...]
    scaled = (hidden.astype(jnp.float32) * gain_ref[...]).astype(jnp.bfloat16)
    both = jnp.concatenate([hidden, scaled], axis=1)
    for y in range(YN):
        for h in range(HN):
            sent_ref[y * HN + h] = both[y * OWN : (y + 1) * OWN]


def project_kernel(info_ref, got_ref, w0, w1, w2, w3, table_ref, k_ref, mix_ref):
    y = info_ref[2]
    total = None
    square = None
    for shift, w in enumerate((w0, w1, w2, w3)):
        source = lax.rem(y + YN - shift, YN)
        part = got_ref[pl.ds(source * HN, HN)].reshape(HN * OWN, 2 * HEAD_DIM)
        term = jnp.dot(part[:, HEAD_DIM:], w[...], preferred_element_type=jnp.float32)
        plain = part[:, :HEAD_DIM].astype(jnp.float32)
        own = jnp.sum(plain * plain, axis=1, keepdims=True)
        total = term if total is None else total + term
        square = own if square is None else square + own
    for s in range(SLOTS):
        part = total[:, s * HEAD_DIM : (s + 1) * HEAD_DIM]
        mix_ref[:, s * OWN : (s + 1) * OWN] = part.reshape(ZN, OWN, HEAD_DIM)
    wide = jnp.broadcast_to(square, (HN * OWN, HEAD_DIM)).reshape(ZN, OWN, HEAD_DIM)
    lane = lax.broadcasted_iota(jnp.int32, (ZN, OWN // 2, HEAD_DIM), 2)
    mix_ref[:, SLOTS * OWN :] = jnp.where(lane < HEAD_DIM // 2, wide[:, : OWN // 2], wide[:, OWN // 2 :])


def turn_kernel(mix_ref, table_ref, queries_ref, new_ref):
    share = mix_ref[0]
    for z in range(1, ZN):
        share = share + mix_ref[z]
    square = share[SLOTS * OWN :]
    half = HEAD_DIM // 2
    inv_rms = lax.rsqrt(jnp.concatenate([square[:, :1], square[:, half : half + 1]], axis=0) / D + 1e-05)
    cosine, sine = table_ref[:, :HEAD_DIM], table_ref[:, HEAD_DIM:]
    slots = []
    for s in range(SLOTS):
        value = share[s * OWN : (s + 1) * OWN] * inv_rms
        if s <= GROUP:
            value = value * cosine + pltpu.roll(value, HEAD_DIM // 2, 1) * sine
        slots.append(value.astype(jnp.bfloat16))
    queries = jnp.concatenate(slots[:GROUP], axis=1)
    for z in range(ZN):
        queries_ref[z] = queries
    new_ref[...] = jnp.concatenate(slots[GROUP:], axis=1)


def packed_levels(level):
    high = level.astype(jnp.bfloat16).astype(jnp.float32)
    mid = (level - high).astype(jnp.bfloat16).astype(jnp.float32)
    low = (level - high) - mid
    return (high + pltpu.roll(mid, GROUP, 1) + pltpu.roll(low, 2 * GROUP, 1)).astype(jnp.bfloat16)


def levels_of(parts):
    parts = parts.astype(jnp.float32)
    level = parts + pltpu.roll(parts, HEAD_DIM - GROUP, 1) + pltpu.roll(parts, HEAD_DIM - 2 * GROUP, 1)
    spot = lax.broadcasted_iota(jnp.int32, parts.shape, 1)
    return jnp.where(spot < GROUP, level, 0.0)


def attend_kernel(shift, info_ref, q_ref, k_ref, v_ref, new_ref, *refs):
    o_ref = refs[-1]
    if len(refs) > 1:
        w_ref, passed_ref, o_ref = refs
        passed_ref[...] = w_ref[...]
    count = info_ref[0]
    first_own = info_ref[1]
    source = lax.rem(info_ref[2] + YN - shift, YN)
    rows = GROUP * SHARE

    def lane(n):
        return lax.broadcasted_iota(jnp.int32, (n, HEAD_DIM), 1)

    def first_lane(n):
        return jnp.where(lane(n) == 0, 1.0, 0.0).astype(jnp.bfloat16)

    def product(a, b):
        return lax.dot_general(a, b, (((1,), (1,)), ((), ())), preferred_element_type=jnp.float32)

    place = lax.broadcasted_iota(jnp.int32, (rows, TAIL), 0) % SHARE
    asked = (place // OWN) * (OWN * YN) + source * OWN + place % OWN
    own = lax.broadcasted_iota(jnp.int32, (rows, TAIL), 1)
    seen = (own < OWN) & (own + first_own <= asked)
    blank = jnp.zeros((TAIL - OWN, HEAD_DIM), jnp.bfloat16)
    tail_keys = jnp.concatenate([new_ref[:, :HEAD_DIM], blank], axis=0)
    tail_values = jnp.concatenate([new_ref[:, HEAD_DIM:], blank], axis=0)
    queries = jnp.concatenate(
        [q_ref[:, :, s * HEAD_DIM : (s + 1) * HEAD_DIM].reshape(SHARE, HEAD_DIM) for s in range(GROUP)], axis=0
    )
    wide = jnp.concatenate([queries, first_lane(rows)], axis=1)
    best = jnp.full((rows, 1), NEG_FILL, jnp.float32)
    sums = jnp.zeros((rows, 2 * HEAD_DIM), jnp.float32)
    for start in range(0, KEYS_DEV + TAIL, KEY_TILE):
        if start < KEYS_DEV:
            index = lax.broadcasted_iota(jnp.int32, (KEY_TILE, HEAD_DIM), 0) + start
            hide = jnp.where((lane(KEY_TILE) == 0) & (index >= count), NEG_FILL, 0.0).astype(jnp.bfloat16)
            keys = jnp.concatenate([k_ref[start : start + KEY_TILE, :], hide], axis=1)
            values = jnp.concatenate([v_ref[start : start + KEY_TILE, :], first_lane(KEY_TILE)], axis=1)
            scores = product(wide, keys)
        else:
            values = jnp.concatenate([tail_values, first_lane(TAIL)], axis=1)
            scores = jnp.where(seen, product(queries, tail_keys), NEG_FILL)
        higher = jnp.maximum(best, jnp.max(scores, axis=1, keepdims=True))
        weights = jnp.exp2((scores - higher) * SCALE2).astype(jnp.bfloat16)
        sums = sums * jnp.exp2((best - higher) * SCALE2) + jnp.dot(
            weights, values, preferred_element_type=jnp.float32
        )
        best = higher
    total = sums[:, HEAD_DIM : HEAD_DIM + 1]
    outs = (sums[:, :HEAD_DIM] * (1.0 / total)).astype(jnp.bfloat16)
    level = best * SCALE + jnp.log(total)
    spot = lane(SHARE)
    levels = jnp.zeros((SHARE, HEAD_DIM), jnp.float32)
    for s in range(GROUP):
        here = slice(s * SHARE, (s + 1) * SHARE)
        o_ref[:, :, s * HEAD_DIM : (s + 1) * HEAD_DIM] = outs[here].reshape(ZN, OWN, HEAD_DIM)
        levels = jnp.where(spot == s, level[here], levels)
    o_ref[:, :, FLAT:] = packed_levels(levels).reshape(ZN, OWN, HEAD_DIM)


def merge_kernel(own_ref, one_ref, two_ref, three_ref, w1, w2, w3, o_ref):
    refs = (own_ref, one_ref, two_ref, three_ref)
    levels = [levels_of(ref[:, :, FLAT:].reshape(SHARE, HEAD_DIM)) for ref in refs]
    most = levels[0]
    for level in levels[1:]:
        most = jnp.maximum(most, level)
    factors = [jnp.exp(level - most) for level in levels]
    total = factors[0] + factors[1] + factors[2] + factors[3]
    factors = [factor * (1.0 / total) for factor in factors]
    for s in range(GROUP):
        here = slice(s * HEAD_DIM, (s + 1) * HEAD_DIM)
        joined = jnp.zeros((SHARE, HEAD_DIM), jnp.float32)
        for ref, factor in zip(refs, factors):
            joined = joined + ref[:, :, here].reshape(SHARE, HEAD_DIM).astype(jnp.float32) * factor[:, s : s + 1]
        o_ref[:, :, here] = joined.astype(jnp.bfloat16).reshape(ZN, OWN, HEAD_DIM)
    spot = lax.broadcasted_iota(jnp.int32, most.shape, 1)
    level = jnp.where(spot < GROUP, most + jnp.log(total), 0.0)
    o_ref[:, :, FLAT:] = packed_levels(level).reshape(ZN, OWN, HEAD_DIM)


def join_kernel(back_ref, rows_ref):
    level = levels_of(back_ref[:, :, FLAT:].reshape(SHARE, HEAD_DIM)).reshape(ZN, OWN, HEAD_DIM)
    factor = jnp.exp(level - jnp.max(level, axis=0, keepdims=True))
    factor = factor * (1.0 / jnp.sum(factor, axis=0, keepdims=True))
    joined = []
    for s in range(GROUP):
        total = jnp.zeros((OWN, HEAD_DIM), jnp.float32)
        for z in range(ZN):
            outs = back_ref[z, :, s * HEAD_DIM : (s + 1) * HEAD_DIM].astype(jnp.float32)
            total = total + outs * factor[z, :, s : s + 1]
        joined.append(total.astype(jnp.bfloat16))
    attended = jnp.concatenate(joined, axis=1)
    for z in range(ZN):
        rows_ref[z] = attended


def finish_kernel(info_ref, rows_ref, w0, w1, w2, w3, o_ref):
    rows = rows_ref[...].reshape(SHARE, FLAT)
    for shift, w in enumerate((w0, w1, w2, w3)):
        source = lax.rem(info_ref[2] + YN - shift, YN)
        term = jnp.dot(rows, w[...], preferred_element_type=jnp.float32)
        o_ref[pl.ds(source * HN, HN)] = term.reshape(HN, OWN, HEAD_DIM)


def rotary_table(positions):
    half = HEAD_DIM // 2
    frequency = 500000.0 ** (-(jnp.arange(half, dtype=jnp.float32) * 2.0 / HEAD_DIM))
    angles = positions.astype(jnp.float32)[:, None] * frequency[None, :]
    cosine, sine = jnp.cos(angles), jnp.sin(angles)
    return jnp.concatenate([cosine, cosine, -sine, sine], axis=1)


def per_device(hidden, norm_gain, w_qkv, positions, cache_keys, cache_values, key_counts, w_out):
    bf16, f32 = jnp.bfloat16, jnp.float32
    y, z = lax.axis_index("y").astype(jnp.int32), lax.axis_index("z").astype(jnp.int32)
    head = lax.axis_index(HEAD).astype(jnp.int32)
    own_columns = lax.dynamic_slice_in_dim(w_qkv, head * WIDTH, WIDTH, axis=1)
    sent = pl.pallas_call(
        split_kernel,
        in_specs=[VMEM, VMEM],
        out_specs=VMEM,
        out_shape=shape((YN * HN, OWN, 2 * HEAD_DIM), bf16),
        compiler_params=params(56),
        name="split",
    )(hidden, norm_gain[None, :])
    columns = [along_y(own_columns, shift) for shift in range(YN)]
    got = exchange(sent, ("y", "x", "core"))
    first_own = z * (OWN * YN) + y * OWN
    info = jnp.stack([key_counts[0], first_own, y])
    table = rotary_table(lax.dynamic_slice_in_dim(positions, first_own, OWN))
    mix = pl.pallas_call(
        project_kernel,
        in_specs=[SMEM] + [VMEM] * 7,
        out_specs=VMEM,
        out_shape=shape((ZN, SLOTS * OWN + OWN // 2, HEAD_DIM), f32),
        compiler_params=params(16),
        name="project",
    )(info, got, *columns, table, cache_keys)
    mix = exchange(mix, "z")
    queries, new_rows = pl.pallas_call(
        turn_kernel,
        in_specs=[VMEM, VMEM],
        out_specs=[VMEM, VMEM],
        out_shape=[shape((ZN, OWN, FLAT), bf16), shape((OWN, 2 * HEAD_DIM), bf16)],
        compiler_params=params(),
        name="turn",
    )(mix, table)
    queries = exchange(queries, "z")
    parts = []
    for shift in range(YN):
        extra = [w_out] if shift == 2 else []
        *passed, part = pl.pallas_call(
            functools.partial(attend_kernel, shift),
            in_specs=[SMEM, VMEM, VMEM, VMEM, VMEM] + [VMEM for _ in extra],
            out_specs=[VMEM for _ in extra] + [VMEM],
            out_shape=[shape(array.shape, bf16) for array in extra] + [shape((ZN, OWN, FLAT + HEAD_DIM), bf16)],
            compiler_params=params(24),
            cost_estimate=pl.CostEstimate(flops=4_000_000_000, bytes_accessed=0, transcendentals=0),
            name="attend",
        )(info, along_y(queries, shift), cache_keys, cache_values, new_rows, *extra)
        if passed:
            w_outs = [w_out] + [along_y(passed[0], step) for step in range(1, YN)]
        parts.append(along_y(part, -shift))
    part = pl.pallas_call(
        merge_kernel,
        in_specs=[VMEM] * 7,
        out_specs=VMEM,
        out_shape=shape((ZN, OWN, FLAT + HEAD_DIM), bf16),
        compiler_params=params(),
        name="merge",
    )(*parts, *w_outs[1:])
    part = exchange(part, "z")
    rows = pl.pallas_call(
        join_kernel,
        in_specs=[VMEM],
        out_specs=VMEM,
        out_shape=shape((ZN, OWN, FLAT), bf16),
        compiler_params=params(),
        name="join",
    )(part)
    rows = exchange(rows, "z")
    result = pl.pallas_call(
        finish_kernel,
        in_specs=[SMEM] + [VMEM] * 5,
        out_specs=VMEM,
        out_shape=shape((YN * HN, OWN, HEAD_DIM), f32),
        compiler_params=params(),
        name="finish",
    )(info, rows, *w_outs)
    result = exchange(result, ("y", "x", "core")).reshape(YN, HN, OWN, HEAD_DIM)
    return jnp.sum(result, axis=1).reshape(YN * OWN, HEAD_DIM).astype(bf16)


def solution(mesh):
    fine = Mesh(mesh.devices.reshape(YN, ZN, XN, CN), ("y", "z", "x", "core"))
    return jax.shard_map(
        per_device,
        mesh=fine,
        in_specs=(
            P(HEAD, CTX),
            P(CTX),
            P(CTX, None),
            P(),
            P(CTX, HEAD),
            P(CTX, HEAD),
            P(CTX),
            P(HEAD, CTX),
        ),
        out_specs=P(HEAD, CTX),
        check_vma=False,
    )
```

```python
import functools
import math

import jax
import jax.numpy as jnp
from jax import lax
from jax.experimental import pallas as pl
from jax.experimental.pallas import tpu as pltpu
from jax.sharding import Mesh
from jax.sharding import PartitionSpec as P

D = 4096
HEADS = 32
KV_HEADS = 8
HEAD_DIM = 128
GROUP = HEADS // KV_HEADS
SLOTS = GROUP + 2
WIDTH = SLOTS * HEAD_DIM
FLAT = GROUP * HEAD_DIM
TQ = 512
KEYS_DEV = 4096
NEG_FILL = -1e30
SCALE = 1.0 / math.sqrt(HEAD_DIM)
SCALE2 = SCALE * 1.4426950408889634

YN, ZN, XN, CN = 4, 8, 4, 2
HN = XN * CN
CTXN = YN * ZN
CTX = ("y", "z")
HEAD = ("x", "core")
OWN = TQ // CTXN
TAIL = 128
KEY_TILE = 512
SHARE = OWN * ZN
RESULT = FLAT + HEAD_DIM

VMEM = pl.BlockSpec(memory_space=pltpu.VMEM)
SMEM = pl.BlockSpec(memory_space=pltpu.SMEM)


def shape(dims, kind):
    return jax.ShapeDtypeStruct(dims, kind)


def params(mib=8):
    return pltpu.CompilerParams(vmem_limit_bytes=mib * 1024 * 1024)


def exchange(array, axes):
    return lax.all_to_all(array, axes, 0, 0, tiled=True)


def along_y(array, shift):
    if shift == 0:
        return array
    return lax.ppermute(array, "y", [(i, (i + shift) % YN) for i in range(YN)])


def split_kernel(hidden_ref, gain_ref, sent_ref):
    hidden = hidden_ref[...]
    scaled = (hidden.astype(jnp.float32) * gain_ref[...]).astype(jnp.bfloat16)
    both = jnp.concatenate([hidden, scaled], axis=1)
    for y in range(YN):
        for h in range(HN):
            sent_ref[y * HN + h] = both[y * OWN : (y + 1) * OWN]


def project_kernel(info_ref, got_ref, w0, w1, w2, w3, table_ref, k_ref, mix_ref):
    y = info_ref[2]
    total = None
    square = None
    for shift, w in enumerate((w0, w1, w2, w3)):
        source = lax.rem(y + YN - shift, YN)
        part = got_ref[pl.ds(source * HN, HN)].reshape(HN * OWN, 2 * HEAD_DIM)
        term = jnp.dot(part[:, HEAD_DIM:], w[...], preferred_element_type=jnp.float32)
        plain = part[:, :HEAD_DIM].astype(jnp.float32)
        own = jnp.sum(plain * plain, axis=1, keepdims=True)
        total = term if total is None else total + term
        square = own if square is None else square + own
    for s in range(SLOTS):
        part = total[:, s * HEAD_DIM : (s + 1) * HEAD_DIM]
        mix_ref[:, s * OWN : (s + 1) * OWN] = part.reshape(ZN, OWN, HEAD_DIM)
    wide = jnp.broadcast_to(square, (HN * OWN, HEAD_DIM)).reshape(ZN, OWN, HEAD_DIM)
    lane = lax.broadcasted_iota(jnp.int32, (ZN, OWN // 2, HEAD_DIM), 2)
    mix_ref[:, SLOTS * OWN :] = jnp.where(lane < HEAD_DIM // 2, wide[:, : OWN // 2], wide[:, OWN // 2 :])


def turn_kernel(mix_ref, table_ref, queries_ref, new_ref):
    share = mix_ref[0]
    for z in range(1, ZN):
        share = share + mix_ref[z]
    square = share[SLOTS * OWN :]
    half = HEAD_DIM // 2
    inv_rms = lax.rsqrt(jnp.concatenate([square[:, :1], square[:, half : half + 1]], axis=0) / D + 1e-05)
    cosine, sine = table_ref[:, :HEAD_DIM], table_ref[:, HEAD_DIM:]
    slots = []
    for s in range(SLOTS):
        value = share[s * OWN : (s + 1) * OWN] * inv_rms
        if s <= GROUP:
            value = value * cosine + pltpu.roll(value, HEAD_DIM // 2, 1) * sine
        slots.append(value.astype(jnp.bfloat16))
    queries = jnp.concatenate(slots[:GROUP], axis=1)
    for z in range(ZN):
        queries_ref[z] = queries
    new_ref[...] = jnp.concatenate(slots[GROUP:], axis=1)


def packed_levels(level):
    high = level.astype(jnp.bfloat16).astype(jnp.float32)
    mid = (level - high).astype(jnp.bfloat16).astype(jnp.float32)
    low = (level - high) - mid
    return (high + pltpu.roll(mid, GROUP, 1) + pltpu.roll(low, 2 * GROUP, 1)).astype(jnp.bfloat16)


def levels_of(parts):
    parts = parts.astype(jnp.float32)
    level = parts + pltpu.roll(parts, HEAD_DIM - GROUP, 1) + pltpu.roll(parts, HEAD_DIM - 2 * GROUP, 1)
    spot = lax.broadcasted_iota(jnp.int32, parts.shape, 1)
    return jnp.where(spot < GROUP, level, 0.0)


def attend_kernel(shift, info_ref, q_ref, k_ref, v_ref, new_ref, *refs):
    o_ref = refs[-1]
    if len(refs) > 1:
        w_ref = refs[0]
        for s in range(GROUP):
            piece = w_ref[s * HEAD_DIM : (s + 1) * HEAD_DIM].reshape(ZN, OWN, HEAD_DIM)
            o_ref[:, :, RESULT + s * HEAD_DIM : RESULT + (s + 1) * HEAD_DIM] = piece
    if len(refs) > 2:
        refs[1][...] = refs[0][...]
    count = info_ref[0]
    first_own = info_ref[1]
    source = lax.rem(info_ref[2] + YN - shift, YN)
    rows = GROUP * SHARE

    def lane(n):
        return lax.broadcasted_iota(jnp.int32, (n, HEAD_DIM), 1)

    def first_lane(n):
        return jnp.where(lane(n) == 0, 1.0, 0.0).astype(jnp.bfloat16)

    def product(a, b):
        return lax.dot_general(a, b, (((1,), (1,)), ((), ())), preferred_element_type=jnp.float32)

    place = lax.broadcasted_iota(jnp.int32, (rows, TAIL), 0) % SHARE
    asked = (place // OWN) * (OWN * YN) + source * OWN + place % OWN
    own = lax.broadcasted_iota(jnp.int32, (rows, TAIL), 1)
    seen = (own < OWN) & (own + first_own <= asked)
    blank = jnp.zeros((TAIL - OWN, HEAD_DIM), jnp.bfloat16)
    tail_keys = jnp.concatenate([new_ref[:, :HEAD_DIM], blank], axis=0)
    tail_values = jnp.concatenate([new_ref[:, HEAD_DIM:], blank], axis=0)
    queries = jnp.concatenate(
        [q_ref[:, :, s * HEAD_DIM : (s + 1) * HEAD_DIM].reshape(SHARE, HEAD_DIM) for s in range(GROUP)], axis=0
    )
    wide = jnp.concatenate([queries, first_lane(rows)], axis=1)
    best = jnp.full((rows, 1), NEG_FILL, jnp.float32)
    sums = jnp.zeros((rows, 2 * HEAD_DIM), jnp.float32)
    for start in range(0, KEYS_DEV + TAIL, KEY_TILE):
        if start < KEYS_DEV // 2:
            values = jnp.concatenate([v_ref[start : start + KEY_TILE, :], first_lane(KEY_TILE)], axis=1)
            scores = product(queries, k_ref[start : start + KEY_TILE, :])
        elif start < KEYS_DEV:
            index = lax.broadcasted_iota(jnp.int32, (KEY_TILE, HEAD_DIM), 0) + start
            hide = jnp.where((lane(KEY_TILE) == 0) & (index >= count), NEG_FILL, 0.0).astype(jnp.bfloat16)
            keys = jnp.concatenate([k_ref[start : start + KEY_TILE, :], hide], axis=1)
            values = jnp.concatenate([v_ref[start : start + KEY_TILE, :], first_lane(KEY_TILE)], axis=1)
            scores = product(wide, keys)
        else:
            values = jnp.concatenate([tail_values, first_lane(TAIL)], axis=1)
            scores = jnp.where(seen, product(queries, tail_keys), NEG_FILL)
        higher = jnp.maximum(best, jnp.max(scores, axis=1, keepdims=True))
        weights = jnp.exp2((scores - higher) * SCALE2).astype(jnp.bfloat16)
        sums = sums * jnp.exp2((best - higher) * SCALE2) + jnp.dot(
            weights, values, preferred_element_type=jnp.float32
        )
        best = higher
    total = sums[:, HEAD_DIM : HEAD_DIM + 1]
    outs = (sums[:, :HEAD_DIM] * (1.0 / total)).astype(jnp.bfloat16)
    level = best * SCALE + jnp.log(total)
    spot = lane(SHARE)
    levels = jnp.zeros((SHARE, HEAD_DIM), jnp.float32)
    for s in range(GROUP):
        here = slice(s * SHARE, (s + 1) * SHARE)
        o_ref[:, :, s * HEAD_DIM : (s + 1) * HEAD_DIM] = outs[here].reshape(ZN, OWN, HEAD_DIM)
        levels = jnp.where(spot == s, level[here], levels)
    o_ref[:, :, FLAT:RESULT] = packed_levels(levels).reshape(ZN, OWN, HEAD_DIM)


def merge_kernel(own_ref, one_ref, two_ref, three_ref, held_ref, o_ref):
    refs = (own_ref, one_ref, two_ref, three_ref)
    levels = [levels_of(ref[:, :, FLAT:RESULT].reshape(SHARE, HEAD_DIM)) for ref in refs]
    most = levels[0]
    for level in levels[1:]:
        most = jnp.maximum(most, level)
    factors = [jnp.exp(level - most) for level in levels]
    total = factors[0] + factors[1] + factors[2] + factors[3]
    factors = [factor * (1.0 / total) for factor in factors]
    for s in range(GROUP):
        here = slice(s * HEAD_DIM, (s + 1) * HEAD_DIM)
        joined = jnp.zeros((SHARE, HEAD_DIM), jnp.float32)
        for ref, factor in zip(refs, factors):
            joined = joined + ref[:, :, here].reshape(SHARE, HEAD_DIM).astype(jnp.float32) * factor[:, s : s + 1]
        o_ref[:, :, here] = joined.astype(jnp.bfloat16).reshape(ZN, OWN, HEAD_DIM)
    spot = lax.broadcasted_iota(jnp.int32, most.shape, 1)
    level = jnp.where(spot < GROUP, most + jnp.log(total), 0.0)
    o_ref[:, :, FLAT:] = packed_levels(level).reshape(ZN, OWN, HEAD_DIM)


def join_kernel(back_ref, rows_ref):
    level = levels_of(back_ref[:, :, FLAT:].reshape(SHARE, HEAD_DIM)).reshape(ZN, OWN, HEAD_DIM)
    factor = jnp.exp(level - jnp.max(level, axis=0, keepdims=True))
    factor = factor * (1.0 / jnp.sum(factor, axis=0, keepdims=True))
    joined = []
    for s in range(GROUP):
        total = jnp.zeros((OWN, HEAD_DIM), jnp.float32)
        for z in range(ZN):
            outs = back_ref[z, :, s * HEAD_DIM : (s + 1) * HEAD_DIM].astype(jnp.float32)
            total = total + outs * factor[z, :, s : s + 1]
        joined.append(total.astype(jnp.bfloat16))
    attended = jnp.concatenate(joined, axis=1)
    for z in range(ZN):
        rows_ref[z] = attended


def finish_kernel(info_ref, rows_ref, w0, three_ref, two_ref, w3, o_ref):
    rows = rows_ref[...].reshape(SHARE, FLAT)

    def carried(ref):
        starts = range(RESULT, RESULT + FLAT, HEAD_DIM)
        return jnp.concatenate([ref[:, :, n : n + HEAD_DIM].reshape(SHARE, HEAD_DIM) for n in starts], axis=0)

    for shift, w in enumerate((w0[...], carried(three_ref), carried(two_ref), w3[...])):
        source = lax.rem(info_ref[2] + YN - shift, YN)
        term = jnp.dot(rows, w, preferred_element_type=jnp.float32)
        o_ref[pl.ds(source * HN, HN)] = term.reshape(HN, OWN, HEAD_DIM)


def rotary_table(positions):
    half = HEAD_DIM // 2
    frequency = 500000.0 ** (-(jnp.arange(half, dtype=jnp.float32) * 2.0 / HEAD_DIM))
    angles = positions.astype(jnp.float32)[:, None] * frequency[None, :]
    cosine, sine = jnp.cos(angles), jnp.sin(angles)
    return jnp.concatenate([cosine, cosine, -sine, sine], axis=1)


def per_device(hidden, norm_gain, w_qkv, positions, cache_keys, cache_values, key_counts, w_out):
    bf16, f32 = jnp.bfloat16, jnp.float32
    y, z = lax.axis_index("y").astype(jnp.int32), lax.axis_index("z").astype(jnp.int32)
    head = lax.axis_index(HEAD).astype(jnp.int32)
    own_columns = lax.dynamic_slice_in_dim(w_qkv, head * WIDTH, WIDTH, axis=1)
    sent = pl.pallas_call(
        split_kernel,
        in_specs=[VMEM, VMEM],
        out_specs=VMEM,
        out_shape=shape((YN * HN, OWN, 2 * HEAD_DIM), bf16),
        compiler_params=params(56),
        name="split",
    )(hidden, norm_gain[None, :])
    columns = [along_y(own_columns, shift) for shift in range(YN)]
    got = exchange(sent, ("y", "x", "core"))
    first_own = z * (OWN * YN) + y * OWN
    info = jnp.stack([key_counts[0], first_own, y])
    table = rotary_table(lax.dynamic_slice_in_dim(positions, first_own, OWN))
    mix = pl.pallas_call(
        project_kernel,
        in_specs=[SMEM] + [VMEM] * 7,
        out_specs=VMEM,
        out_shape=shape((ZN, SLOTS * OWN + OWN // 2, HEAD_DIM), f32),
        compiler_params=params(16),
        name="project",
    )(info, got, *columns, table, cache_keys)
    mix = exchange(mix, "z")
    queries, new_rows = pl.pallas_call(
        turn_kernel,
        in_specs=[VMEM, VMEM],
        out_specs=[VMEM, VMEM],
        out_shape=[shape((ZN, OWN, FLAT), bf16), shape((OWN, 2 * HEAD_DIM), bf16)],
        compiler_params=params(),
        name="turn",
    )(mix, table)
    queries = exchange(queries, "z")
    parts = []
    for shift in range(YN):
        carries = shift in (2, 3)
        outs = [shape((ZN, OWN, RESULT + (FLAT if carries else 0)), bf16)]
        if shift == 2:
            outs.insert(0, shape(w_out.shape, bf16))
        *passed, part = pl.pallas_call(
            functools.partial(attend_kernel, shift),
            in_specs=[SMEM] + [VMEM] * (5 if carries else 4),
            out_specs=[VMEM for _ in outs],
            out_shape=outs,
            compiler_params=params(24),
            cost_estimate=pl.CostEstimate(flops=4_000_000_000, bytes_accessed=0, transcendentals=0),
            name="attend",
        )(info, along_y(queries, shift), cache_keys, cache_values, new_rows, *([w_out] if carries else []))
        if passed:
            last_columns = along_y(passed[0], 3)
        parts.append(along_y(part, -shift))
    part = pl.pallas_call(
        merge_kernel,
        in_specs=[VMEM] * 5,
        out_specs=VMEM,
        out_shape=shape((ZN, OWN, FLAT + HEAD_DIM), bf16),
        compiler_params=params(),
        name="merge",
    )(*parts, last_columns)
    part = exchange(part, "z")
    rows = pl.pallas_call(
        join_kernel,
        in_specs=[VMEM],
        out_specs=VMEM,
        out_shape=shape((ZN, OWN, FLAT), bf16),
        compiler_params=params(),
        name="join",
    )(part)
    rows = exchange(rows, "z")
    result = pl.pallas_call(
        finish_kernel,
        in_specs=[SMEM] + [VMEM] * 5,
        out_specs=VMEM,
        out_shape=shape((YN * HN, OWN, HEAD_DIM), f32),
        compiler_params=params(),
        name="finish",
    )(info, rows, w_out, parts[3], parts[2], last_columns)
    result = exchange(result, ("y", "x", "core")).reshape(YN, HN, OWN, HEAD_DIM)
    return jnp.sum(result, axis=1).reshape(YN * OWN, HEAD_DIM).astype(bf16)


def solution(mesh):
    fine = Mesh(mesh.devices.reshape(YN, ZN, XN, CN), ("y", "z", "x", "core"))
    return jax.shard_map(
        per_device,
        mesh=fine,
        in_specs=(
            P(HEAD, CTX),
            P(CTX),
            P(CTX, None),
            P(),
            P(CTX, HEAD),
            P(CTX, HEAD),
            P(CTX),
            P(HEAD, CTX),
        ),
        out_specs=P(HEAD, CTX),
        check_vma=False,
    )
```

```python
import functools
import math

import jax
import jax.numpy as jnp
from jax import lax
from jax.experimental import pallas as pl
from jax.experimental.pallas import tpu as pltpu
from jax.sharding import Mesh
from jax.sharding import PartitionSpec as P

D = 4096
HEADS = 32
KV_HEADS = 8
HEAD_DIM = 128
GROUP = HEADS // KV_HEADS
SLOTS = GROUP + 2
WIDTH = SLOTS * HEAD_DIM
FLAT = GROUP * HEAD_DIM
TQ = 512
KEYS_DEV = 4096
NEG_FILL = -1e30
SCALE = 1.0 / math.sqrt(HEAD_DIM)
SCALE2 = SCALE * 1.4426950408889634

YN, ZN, XN, CN = 4, 8, 4, 2
HN = XN * CN
CTXN = YN * ZN
CTX = ("y", "z")
HEAD = ("x", "core")
OWN = TQ // CTXN
TAIL = 128
KEY_TILE = 512
SHARE = OWN * ZN
RESULT = FLAT + HEAD_DIM

VMEM = pl.BlockSpec(memory_space=pltpu.VMEM)
SMEM = pl.BlockSpec(memory_space=pltpu.SMEM)


def shape(dims, kind):
    return jax.ShapeDtypeStruct(dims, kind)


def params(mib=8):
    return pltpu.CompilerParams(vmem_limit_bytes=mib * 1024 * 1024)


def exchange(array, axes):
    return lax.all_to_all(array, axes, 0, 0, tiled=True)


def along_y(array, shift):
    if shift == 0:
        return array
    return lax.ppermute(array, "y", [(i, (i + shift) % YN) for i in range(YN)])


def split_kernel(hidden_ref, gain_ref, sent_ref):
    hidden = hidden_ref[...]
    scaled = (hidden.astype(jnp.float32) * gain_ref[...]).astype(jnp.bfloat16)
    both = jnp.concatenate([hidden, scaled], axis=1)
    for y in range(YN):
        for h in range(HN):
            sent_ref[y * HN + h] = both[y * OWN : (y + 1) * OWN]


def project_kernel(info_ref, got_ref, w0, w1, w2, w3, table_ref, k_ref, mix_ref):
    y = info_ref[2]
    total = None
    square = None
    for shift, w in enumerate((w0, w1, w2, w3)):
        source = lax.rem(y + YN - shift, YN)
        part = got_ref[pl.ds(source * HN, HN)].reshape(HN * OWN, 2 * HEAD_DIM)
        term = jnp.dot(part[:, HEAD_DIM:], w[...], preferred_element_type=jnp.float32)
        plain = part[:, :HEAD_DIM].astype(jnp.float32)
        own = jnp.sum(plain * plain, axis=1, keepdims=True)
        total = term if total is None else total + term
        square = own if square is None else square + own
    for s in range(SLOTS):
        part = total[:, s * HEAD_DIM : (s + 1) * HEAD_DIM]
        mix_ref[:, s * OWN : (s + 1) * OWN] = part.reshape(ZN, OWN, HEAD_DIM)
    wide = jnp.broadcast_to(square, (HN * OWN, HEAD_DIM)).reshape(ZN, OWN, HEAD_DIM)
    lane = lax.broadcasted_iota(jnp.int32, (ZN, OWN // 2, HEAD_DIM), 2)
    mix_ref[:, SLOTS * OWN :] = jnp.where(lane < HEAD_DIM // 2, wide[:, : OWN // 2], wide[:, OWN // 2 :])


def turn_kernel(mix_ref, table_ref, queries_ref, new_ref):
    share = mix_ref[0]
    for z in range(1, ZN):
        share = share + mix_ref[z]
    square = share[SLOTS * OWN :]
    half = HEAD_DIM // 2
    inv_rms = lax.rsqrt(jnp.concatenate([square[:, :1], square[:, half : half + 1]], axis=0) / D + 1e-05)
    cosine, sine = table_ref[:, :HEAD_DIM], table_ref[:, HEAD_DIM:]
    slots = []
    for s in range(SLOTS):
        value = share[s * OWN : (s + 1) * OWN] * inv_rms
        if s <= GROUP:
            value = value * cosine + pltpu.roll(value, HEAD_DIM // 2, 1) * sine
        slots.append(value.astype(jnp.bfloat16))
    queries = jnp.concatenate(slots[:GROUP], axis=1)
    for z in range(ZN):
        queries_ref[z] = queries
    new_ref[...] = jnp.concatenate(slots[GROUP:], axis=1)


def packed_levels(level):
    high = level.astype(jnp.bfloat16).astype(jnp.float32)
    mid = (level - high).astype(jnp.bfloat16).astype(jnp.float32)
    low = (level - high) - mid
    return (high + pltpu.roll(mid, GROUP, 1) + pltpu.roll(low, 2 * GROUP, 1)).astype(jnp.bfloat16)


def levels_of(parts):
    parts = parts.astype(jnp.float32)
    level = parts + pltpu.roll(parts, HEAD_DIM - GROUP, 1) + pltpu.roll(parts, HEAD_DIM - 2 * GROUP, 1)
    spot = lax.broadcasted_iota(jnp.int32, parts.shape, 1)
    return jnp.where(spot < GROUP, level, 0.0)


def attend_kernel(shift, info_ref, q_ref, k_ref, v_ref, new_ref, *refs):
    o_ref = refs[-1]
    if len(refs) > 2:
        w_ref = refs[0]
        for s in range(GROUP):
            piece = w_ref[s * HEAD_DIM : (s + 1) * HEAD_DIM].reshape(ZN, OWN, HEAD_DIM)
            o_ref[:, :, RESULT + s * HEAD_DIM : RESULT + (s + 1) * HEAD_DIM] = piece
    if len(refs) > 2:
        refs[1][...] = refs[0][...]
    count = info_ref[0]
    first_own = info_ref[1]
    source = lax.rem(info_ref[2] + YN - shift, YN)
    rows = GROUP * SHARE

    def lane(n):
        return lax.broadcasted_iota(jnp.int32, (n, HEAD_DIM), 1)

    def first_lane(n):
        return jnp.where(lane(n) == 0, 1.0, 0.0).astype(jnp.bfloat16)

    def product(a, b):
        return lax.dot_general(a, b, (((1,), (1,)), ((), ())), preferred_element_type=jnp.float32)

    place = lax.broadcasted_iota(jnp.int32, (rows, TAIL), 0) % SHARE
    asked = (place // OWN) * (OWN * YN) + source * OWN + place % OWN
    own = lax.broadcasted_iota(jnp.int32, (rows, TAIL), 1)
    seen = (own < OWN) & (own + first_own <= asked)
    blank = jnp.zeros((TAIL - OWN, HEAD_DIM), jnp.bfloat16)
    tail_keys = jnp.concatenate([new_ref[:, :HEAD_DIM], blank], axis=0)
    tail_values = jnp.concatenate([new_ref[:, HEAD_DIM:], blank], axis=0)
    queries = jnp.concatenate(
        [q_ref[:, :, s * HEAD_DIM : (s + 1) * HEAD_DIM].reshape(SHARE, HEAD_DIM) for s in range(GROUP)], axis=0
    )
    wide = jnp.concatenate([queries, first_lane(rows)], axis=1)
    best = jnp.full((rows, 1), NEG_FILL, jnp.float32)
    sums = jnp.zeros((rows, 2 * HEAD_DIM), jnp.float32)
    for start in range(0, KEYS_DEV + TAIL, KEY_TILE):
        if start < KEYS_DEV // 2:
            values = jnp.concatenate([v_ref[start : start + KEY_TILE, :], first_lane(KEY_TILE)], axis=1)
            scores = product(queries, k_ref[start : start + KEY_TILE, :])
        elif start < KEYS_DEV:
            index = lax.broadcasted_iota(jnp.int32, (KEY_TILE, HEAD_DIM), 0) + start
            hide = jnp.where((lane(KEY_TILE) == 0) & (index >= count), NEG_FILL, 0.0).astype(jnp.bfloat16)
            keys = jnp.concatenate([k_ref[start : start + KEY_TILE, :], hide], axis=1)
            values = jnp.concatenate([v_ref[start : start + KEY_TILE, :], first_lane(KEY_TILE)], axis=1)
            scores = product(wide, keys)
        else:
            values = jnp.concatenate([tail_values, first_lane(TAIL)], axis=1)
            scores = jnp.where(seen, product(queries, tail_keys), NEG_FILL)
        higher = jnp.maximum(best, jnp.max(scores, axis=1, keepdims=True))
        weights = jnp.exp2((scores - higher) * SCALE2).astype(jnp.bfloat16)
        sums = sums * jnp.exp2((best - higher) * SCALE2) + jnp.dot(
            weights, values, preferred_element_type=jnp.float32
        )
        best = higher
    total = sums[:, HEAD_DIM : HEAD_DIM + 1]
    outs = (sums[:, :HEAD_DIM] * (1.0 / total)).astype(jnp.bfloat16)
    level = best * SCALE + jnp.log(total)
    spot = lane(SHARE)
    levels = jnp.zeros((SHARE, HEAD_DIM), jnp.float32)
    for s in range(GROUP):
        here = slice(s * SHARE, (s + 1) * SHARE)
        o_ref[:, :, s * HEAD_DIM : (s + 1) * HEAD_DIM] = outs[here].reshape(ZN, OWN, HEAD_DIM)
        levels = jnp.where(spot == s, level[here], levels)
    o_ref[:, :, FLAT:RESULT] = packed_levels(levels).reshape(ZN, OWN, HEAD_DIM)


def merge_kernel(own_ref, one_ref, two_ref, three_ref, held_ref, o_ref):
    refs = (own_ref, one_ref, two_ref, three_ref)
    levels = [levels_of(ref[:, :, FLAT:RESULT].reshape(SHARE, HEAD_DIM)) for ref in refs]
    most = levels[0]
    for level in levels[1:]:
        most = jnp.maximum(most, level)
    factors = [jnp.exp(level - most) for level in levels]
    total = factors[0] + factors[1] + factors[2] + factors[3]
    factors = [factor * (1.0 / total) for factor in factors]
    for s in range(GROUP):
        here = slice(s * HEAD_DIM, (s + 1) * HEAD_DIM)
        joined = jnp.zeros((SHARE, HEAD_DIM), jnp.float32)
        for ref, factor in zip(refs, factors):
            joined = joined + ref[:, :, here].reshape(SHARE, HEAD_DIM).astype(jnp.float32) * factor[:, s : s + 1]
        o_ref[:, :, here] = joined.astype(jnp.bfloat16).reshape(ZN, OWN, HEAD_DIM)
    spot = lax.broadcasted_iota(jnp.int32, most.shape, 1)
    level = jnp.where(spot < GROUP, most + jnp.log(total), 0.0)
    o_ref[:, :, FLAT:] = packed_levels(level).reshape(ZN, OWN, HEAD_DIM)


def join_kernel(back_ref, rows_ref):
    level = levels_of(back_ref[:, :, FLAT:].reshape(SHARE, HEAD_DIM)).reshape(ZN, OWN, HEAD_DIM)
    factor = jnp.exp(level - jnp.max(level, axis=0, keepdims=True))
    factor = factor * (1.0 / jnp.sum(factor, axis=0, keepdims=True))
    joined = []
    for s in range(GROUP):
        total = jnp.zeros((OWN, HEAD_DIM), jnp.float32)
        for z in range(ZN):
            outs = back_ref[z, :, s * HEAD_DIM : (s + 1) * HEAD_DIM].astype(jnp.float32)
            total = total + outs * factor[z, :, s : s + 1]
        joined.append(total.astype(jnp.bfloat16))
    attended = jnp.concatenate(joined, axis=1)
    for z in range(ZN):
        rows_ref[z] = attended


def finish_kernel(info_ref, rows_ref, w0, three_ref, two_ref, w3, o_ref):
    rows = rows_ref[...].reshape(SHARE, FLAT)

    def carried(ref):
        starts = range(RESULT, RESULT + FLAT, HEAD_DIM)
        return jnp.concatenate([ref[:, :, n : n + HEAD_DIM].reshape(SHARE, HEAD_DIM) for n in starts], axis=0)

    for shift, w in enumerate((w0[...], carried(three_ref), carried(two_ref), w3[...])):
        source = lax.rem(info_ref[2] + YN - shift, YN)
        term = jnp.dot(rows, w, preferred_element_type=jnp.float32)
        o_ref[pl.ds(source * HN, HN)] = term.reshape(HN, OWN, HEAD_DIM)


def rotary_table(positions):
    half = HEAD_DIM // 2
    frequency = 500000.0 ** (-(jnp.arange(half, dtype=jnp.float32) * 2.0 / HEAD_DIM))
    angles = positions.astype(jnp.float32)[:, None] * frequency[None, :]
    cosine, sine = jnp.cos(angles), jnp.sin(angles)
    return jnp.concatenate([cosine, cosine, -sine, sine], axis=1)


def per_device(hidden, norm_gain, w_qkv, positions, cache_keys, cache_values, key_counts, w_out):
    bf16, f32 = jnp.bfloat16, jnp.float32
    y, z = lax.axis_index("y").astype(jnp.int32), lax.axis_index("z").astype(jnp.int32)
    head = lax.axis_index(HEAD).astype(jnp.int32)
    own_columns = lax.dynamic_slice_in_dim(w_qkv, head * WIDTH, WIDTH, axis=1)
    sent = pl.pallas_call(
        split_kernel,
        in_specs=[VMEM, VMEM],
        out_specs=VMEM,
        out_shape=shape((YN * HN, OWN, 2 * HEAD_DIM), bf16),
        compiler_params=params(56),
        name="split",
    )(hidden, norm_gain[None, :])
    columns = [along_y(own_columns, shift) for shift in range(YN)]
    got = exchange(sent, ("y", "x", "core"))
    first_own = z * (OWN * YN) + y * OWN
    info = jnp.stack([key_counts[0], first_own, y])
    table = rotary_table(lax.dynamic_slice_in_dim(positions, first_own, OWN))
    mix = pl.pallas_call(
        project_kernel,
        in_specs=[SMEM] + [VMEM] * 7,
        out_specs=VMEM,
        out_shape=shape((ZN, SLOTS * OWN + OWN // 2, HEAD_DIM), f32),
        compiler_params=params(16),
        name="project",
    )(info, got, *columns, table, cache_keys)
    mix = exchange(mix, "z")
    queries, new_rows = pl.pallas_call(
        turn_kernel,
        in_specs=[VMEM, VMEM],
        out_specs=[VMEM, VMEM],
        out_shape=[shape((ZN, OWN, FLAT), bf16), shape((OWN, 2 * HEAD_DIM), bf16)],
        compiler_params=params(),
        name="turn",
    )(mix, table)
    queries = exchange(queries, "z")
    parts, handed = {}, [w_out]
    for shift in (2, 3, 1, 0):
        carries = shift in (2, 3)
        outs = [shape((ZN, OWN, RESULT + (FLAT if carries else 0)), bf16)]
        if carries:
            outs.insert(0, shape(w_out.shape, bf16))
        extra = handed[-1:] if shift else [last_columns]
        *passed, part = pl.pallas_call(
            functools.partial(attend_kernel, shift),
            in_specs=[SMEM] + [VMEM] * (4 + len(extra)),
            out_specs=[VMEM for _ in outs],
            out_shape=outs,
            compiler_params=params(24),
            cost_estimate=pl.CostEstimate(flops=1000000000, bytes_accessed=0, transcendentals=0),
            name="attend",
        )(info, along_y(queries, shift), cache_keys, cache_values, new_rows, *extra)
        handed.extend(passed)
        if shift == 2:
            last_columns = along_y(passed[0], 3)
        parts[shift] = along_y(part, -shift)
    part = pl.pallas_call(
        merge_kernel,
        in_specs=[VMEM] * 5,
        out_specs=VMEM,
        out_shape=shape((ZN, OWN, FLAT + HEAD_DIM), bf16),
        compiler_params=params(),
        name="merge",
    )(*[parts[shift] for shift in range(YN)], last_columns)
    part = exchange(part, "z")
    rows = pl.pallas_call(
        join_kernel,
        in_specs=[VMEM],
        out_specs=VMEM,
        out_shape=shape((ZN, OWN, FLAT), bf16),
        compiler_params=params(),
        name="join",
    )(part)
    rows = exchange(rows, "z")
    result = pl.pallas_call(
        finish_kernel,
        in_specs=[SMEM] + [VMEM] * 5,
        out_specs=VMEM,
        out_shape=shape((YN * HN, OWN, HEAD_DIM), f32),
        compiler_params=params(),
        name="finish",
    )(info, rows, w_out, parts[3], parts[2], last_columns)
    result = exchange(result, ("y", "x", "core")).reshape(YN, HN, OWN, HEAD_DIM)
    return jnp.sum(result, axis=1).reshape(YN * OWN, HEAD_DIM).astype(bf16)


def solution(mesh):
    fine = Mesh(mesh.devices.reshape(YN, ZN, XN, CN), ("y", "z", "x", "core"))
    return jax.shard_map(
        per_device,
        mesh=fine,
        in_specs=(
            P(HEAD, CTX),
            P(CTX),
            P(CTX, None),
            P(),
            P(CTX, HEAD),
            P(CTX, HEAD),
            P(CTX),
            P(HEAD, CTX),
        ),
        out_specs=P(HEAD, CTX),
        check_vma=False,
    )
```
